512 devices in a mesh: tile: 128 (over z, y, core), panel: 4 (over x).
Axes of the slice: x: 4, y: 8, z: 8, core: 2. Of those that a mesh axis runs over, the one named last changes fastest.
Arguments:
- reconstructor: bfloat16 [128, 30720], P('panel', 'tile'), may hold values from -6 to 6
- c_as: bfloat16 [128, 30720], P('panel', 'tile'), may hold values from -6 to 6
- tiles: bfloat16 [128, 2048, 2048], P('tile', 'panel'), may hold values from -0.03125 to 0.03125
- tile_pairs: int32 [120, 2], replicated, may hold values from 0 to 14, as said below
- tile_slot: int32 [120], replicated, may hold values from 0 to 127, as said below
Outputs:
- grad_out: float32 [128, 30720], P('panel', 'tile')
The draws below stay inside these ranges and needn't reach their ends.
Inputs may be any that keep to these rules, and one draw needn't show every extreme that they name: `tile_pairs`: each pair (a, b) with b <= a < 15 appears exactly once. `tile_slot`: distinct slots; slot s belongs to index s // 1 of tile; each index of tile holds one slot; 120 of the 128 slots are used, slots 0 and 127 always among them.
All inputs are finite; a program needn't handle non-finite values.
Results may differ from the reference program's by a relative error of at most 0.0003.
Values may be sent and summed in bfloat16 or wider, within the bound.
A program may use at most 64 MiB of HBM per device.

```python
import jax
import jax.numpy as jnp
from jax import lax

TS = 2048
SLOPES = 30720
NB = 15
TILES = 120
TILE_DEV = 1
SLOTS = 128
ACT = 128
N_TILE = 128


def draw_tile_pairs(key, part):
    key = jax.random.fold_in(key, 11)
    order = jax.random.permutation(key, TILES).astype(jnp.int32)
    levels = jnp.arange(NB, dtype=jnp.int32)
    triangle = levels * (levels + 1) // 2
    lower_block = jnp.sum((triangle[None, :] <= order[:, None]).astype(jnp.int32), axis=1) - 1
    upper_block = order - lower_block * (lower_block + 1) // 2
    return jnp.stack([lower_block, upper_block], axis=1).astype(jnp.int32)


def draw_tile_slot(key, part):
    key = jax.random.fold_in(key, 12)
    key_device, key_order = jax.random.split(key)
    chosen = jax.random.randint(key_device, (), 0, N_TILE).astype(jnp.int32)
    slot_ids = jnp.arange(SLOTS, dtype=jnp.int32)
    shuffled = jax.random.permutation(key_order, SLOTS).astype(jnp.int32)
    first_use = (slot_ids // TILE_DEV == chosen) | (slot_ids == 0) | (slot_ids == SLOTS - 1)
    scores = jnp.where(first_use, slot_ids, SLOTS + shuffled)
    ranking = jnp.argsort(scores, stable=True).astype(jnp.int32)
    return ranking[:TILES]


def block_levels(stream_key, extent, cuts, least, largest):
    def one(dim, blocks):
        heights = jax.random.uniform(jax.random.fold_in(jax.random.fold_in(stream_key, 6), dim), (blocks,), jnp.float32, least / len(cuts), largest / len(cuts))
        return jnp.repeat(jnp.exp(heights), extent[dim] // blocks).reshape((-1,) + (1,) * (len(extent) - dim - 1))

    factor_of = one(*cuts[0])
    for cut in cuts[1:]:
        factor_of = factor_of * one(*cut)
    return factor_of


def centred(key, extent, scale, most, shards=(), kind=jnp.bfloat16):
    gain = block_levels(key, extent, shards, -0.22, 0.18) if shards else 1.0
    drawn = jax.random.normal(key, extent, jnp.float32) * scale * gain
    return jnp.minimum(jnp.maximum(drawn, -most), most).astype(kind)


def setup_inputs(seed: int = 0) -> dict:
    key_list = jax.random.split(jax.random.key(seed), 6)
    return {
        "reconstructor": centred(key_list[0], (ACT, SLOPES), 1.0, 6.0, ((0, 4), (1, 128))),
        "c_as": centred(key_list[1], (ACT, SLOPES), 1.0, 6.0, ((0, 4), (1, 128))),
        "tiles": centred(key_list[2], (SLOTS, TS, TS), SLOPES ** -0.5, 0.03125, ((0, 128), (1, 4))),
        "tile_pairs": draw_tile_pairs(jax.random.fold_in(key_list[5], 71), 0),
        "tile_slot": draw_tile_slot(jax.random.fold_in(key_list[5], 71), 0),
    }


def reference(reconstructor, c_as, tiles, tile_pairs, tile_slot):
    act_rows = reconstructor.shape[0]

    def accumulate(running, tile_index):
        lower_block = tile_pairs[tile_index, 0].astype(jnp.int32)
        upper_block = tile_pairs[tile_index, 1].astype(jnp.int32)
        one_tile = lax.dynamic_index_in_dim(tiles, tile_slot[tile_index].astype(jnp.int32), 0, keepdims=False)
        factor = jnp.where(lower_block == upper_block, 0.5, 1.0).astype(jnp.float32)
        rows_lower = lax.dynamic_slice_in_dim(reconstructor, lower_block * TS, TS, 1)
        rows_upper = lax.dynamic_slice_in_dim(reconstructor, upper_block * TS, TS, 1)
        direct = jnp.dot(rows_lower, one_tile, preferred_element_type=jnp.float32) * factor
        mirrored = jnp.dot(rows_upper, one_tile.T, preferred_element_type=jnp.float32) * factor
        current = lax.dynamic_slice_in_dim(running, upper_block * TS, TS, 1)
        running = lax.dynamic_update_slice_in_dim(running, current + direct, upper_block * TS, 1)
        current = lax.dynamic_slice_in_dim(running, lower_block * TS, TS, 1)
        running = lax.dynamic_update_slice_in_dim(running, current + mirrored, lower_block * TS, 1)
        return running, None

    running, _ = lax.scan(accumulate, jnp.zeros((act_rows, SLOPES), jnp.float32), jnp.arange(TILES, dtype=jnp.int32))
    return 2.0 * (running - c_as.astype(jnp.float32))
```

```python
import functools

import jax
import jax.numpy as jnp
from jax import lax
from jax.experimental import pallas as pl
from jax.experimental.pallas import tpu as pltpu
from jax.sharding import PartitionSpec as P

MESH = pl.DeviceIdType.MESH
L = 128
F32 = jnp.float32
BF16 = jnp.bfloat16


def wait_for(ref, sem):
    pltpu.make_async_copy(ref, ref, sem).wait()


def kernel(
    cfg,
    pairs_ref, slot_ref, r_ref, x_hbm,
    out_ref,
    xv, img, c_in, own, gath, s3s, afull, aop, bop, dbuf, mbuf, drecv, dsum, mfull, part, acc, q_in, f_own, o_in, tab,
    x_sem, s1s, s1r, s2s, s2r, s3sa, s3ra, s4as, s4ar, s4bs, s4br, ds, dr, ms, mr, ps, pr, qs, qr, os_, or_,
):
    A, W, NX, NZ, NP, NB, T = cfg
    TS = NP * L
    H = TS // NX
    CP = NP * W // L
    G = NX
    GL = TS // G
    GC = NP // G
    t = lax.axis_index("tile")
    p = lax.axis_index("panel")
    z = t // NP
    j = t % NP

    def plane(i):
        return {"tile": z * NP + i}

    def along_z(zz):
        return {"tile": zz * NP + j}

    def along_x(pp):
        return {"panel": pp}

    def send(src, dst, ssem, rsem, dev):
        pltpu.make_async_remote_copy(
            src_ref=src, dst_ref=dst, send_sem=ssem, recv_sem=rsem, device_id=dev, device_id_type=MESH
        ).start()

    x_copy = pltpu.make_async_copy(x_hbm.at[0], xv, x_sem)
    x_copy.start()

    c_in[...] = jnp.zeros_like(c_in)
    o_in[...] = jnp.zeros_like(o_in)
    h0 = (W * j) // L
    off = W * j - L * h0
    row = lax.broadcasted_iota(jnp.int32, (W, 3 * L), 0)
    col = lax.broadcasted_iota(jnp.int32, (W, 3 * L), 1)
    shift = jnp.where(col - row == off, 1.0, 0.0).astype(BF16)
    placed = jnp.dot(r_ref[...], shift, preferred_element_type=F32).astype(BF16)
    for s in range(3):
        img[s] = placed[:, s * L : (s + 1) * L]

    barrier = pltpu.get_barrier_semaphore()

    @pl.loop(1, NP)
    def _(d):
        pl.semaphore_signal(barrier, inc=1, device_id=plane((j + d) % NP), device_id_type=MESH)

    @pl.loop(1, NZ)
    def _(d):
        pl.semaphore_signal(barrier, inc=1, device_id=along_z((z + d) % NZ), device_id_type=MESH)

    @pl.loop(1, NX)
    def _(d):
        pl.semaphore_signal(barrier, inc=1, device_id=along_x((p + d) % NX), device_id_type=MESH)

    pl.semaphore_wait(barrier, NP + NZ + NX - 3)

    for s in range(3):
        h = h0 + s
        live = L * h < W * (j + 1)
        dest = (CP * z + h) % NP
        e = h // NP
        c = jnp.where((off > 0) & (s == 0), 1, 0)

        @pl.when(live & (dest == j))
        def _():
            c_in[e, c] = img[s]

        @pl.when(live & (dest != j))
        def _():
            send(img.at[s], c_in.at[e, c], s1s.at[s], s1r.at[e, c], plane(dest))

    def look(n, got):
        slot = slot_ref[n]
        code = pairs_ref[0, n] * 16 + pairs_ref[1, n]
        return tuple(jnp.where(slot == z * NP + i, code, got[i]) for i in range(NP))

    found = lax.fori_loop(0, T, look, tuple(jnp.int32(-1) for _ in range(NP)))
    mine = jnp.int32(-1)
    for i in range(NP):
        known = jnp.maximum(found[i], 0)
        tab[0, i] = known // 16
        tab[1, i] = known % 16
        mine = jnp.where(j == i, found[i], mine)
    diag = jnp.where(mine // 16 == mine % 16, 0.5, 1.0)
    factor = jnp.where(mine < 0, 0.0, diag).astype(F32)

    hp = (j + (NP - CP % NP) * z) % NP
    for e in range(2):
        h = hp + NP * e
        i_lo = (L * h) // W
        i_hi = (L * h + L - 1) // W

        @pl.when((h < CP) & (i_lo != j))
        def _():
            wait_for(c_in.at[e, 0], s1r.at[e, 0])

        @pl.when((h < CP) & (i_hi != i_lo) & (i_hi != j))
        def _():
            wait_for(c_in.at[e, 1], s1r.at[e, 1])

        mix = (c_in[e, 0].astype(F32) + c_in[e, 1].astype(F32)).astype(BF16)
        own[e] = mix
        gath[2 * z + e] = mix

    @pl.loop(1, NZ)
    def _(d):
        zz = (z + d) % NZ
        send(own, gath.at[pl.ds(2 * z, 2)], s2s.at[d], s2r.at[z], along_z(zz))

    @pl.loop(1, NZ)
    def _(d):
        zz = (z + NZ - d) % NZ
        wait_for(gath.at[pl.ds(2 * zz, 2)], s2r.at[zz])

    p_rows = pl.ds(pl.multiple_of(p * A, A), A)

    def chunk_of(which, i):
        g = tab[which, i] * NP + j
        return gath[2 * (g // CP) + (g % CP) // NP]

    j_lanes = pl.ds(pl.multiple_of(j * L, L), L)
    for which in range(2):

        @pl.loop(1, NP)
        def _(d):
            i = (j + d) % NP
            s3s[which, d] = chunk_of(which, i)
            dst = afull.at[:, j_lanes] if which == 0 else bop.at[p_rows, j_lanes]
            send(s3s.at[which, d], dst, s3sa.at[which, d], s3ra.at[which, j], plane(i))

    afull[:, j_lanes] = chunk_of(0, j)
    bop[p_rows, j_lanes] = chunk_of(1, j)

    @pl.loop(1, NP)
    def _(d):
        i = (j + d) % NP
        wait_for(afull.at[:, pl.ds(pl.multiple_of(i * L, L), L)], s3ra.at[0, i])

    @pl.loop(1, NX)
    def _(d):
        pp = (p + d) % NX
        send(
            afull.at[:, pl.ds(pl.multiple_of(pp * H, H), H)], aop.at[p_rows, :], s4as.at[d], s4ar.at[p], along_x(pp)
        )

    aop[p_rows, :] = afull[:, pl.ds(pl.multiple_of(p * H, H), H)]

    @pl.loop(0, G)
    def _(q):
        @pl.loop(0, GC)
        def _(n):
            i = q * GC + n

            @pl.when(i != j)
            def _():
                wait_for(bop.at[p_rows, pl.ds(pl.multiple_of(i * L, L), L)], s3ra.at[1, i])

        lanes = pl.ds(pl.multiple_of(q * GL, GL), GL)

        @pl.loop(1, NX)
        def _(d):
            pp = (p + d) % NX
            send(bop.at[p_rows, lanes], bop.at[p_rows, lanes], s4bs.at[q, d], s4br.at[q, p], along_x(pp))

    @pl.loop(1, NX)
    def _(d):
        pp = (p + d) % NX
        wait_for(aop.at[pl.ds(pl.multiple_of(pp * A, A), A), :], s4ar.at[pp])

    x_copy.wait()

    @pl.loop(0, G)
    def _(q):
        lanes = pl.ds(pl.multiple_of(q * GL, GL), GL)
        dbuf[q] = jnp.dot(aop[...], xv[:, lanes], preferred_element_type=F32) * factor

        @pl.loop(1, NX)
        def _(d):
            pp = (p + d) % NX
            rows = pl.ds(pl.multiple_of(pp * A, A), A)
            send(dbuf.at[q, rows, :], drecv.at[p, q], ds.at[q, d], dr.at[q, p], along_x(pp))

    mbuf[...] = jnp.zeros_like(mbuf)

    @pl.loop(0, G)
    def _(q):
        lanes = pl.ds(pl.multiple_of(q * GL, GL), GL)

        @pl.loop(1, NX)
        def _(d):
            pp = (p + d) % NX
            wait_for(bop.at[pl.ds(pl.multiple_of(pp * A, A), A), lanes], s4br.at[q, pp])

        mbuf[...] += lax.dot_general(
            bop[:, lanes], xv[:, lanes], (((1,), (1,)), ((), ())), preferred_element_type=F32
        )

    mbuf[...] = mbuf[...] * factor
    p_cols = pl.ds(pl.multiple_of(p * H, H), H)

    @pl.loop(1, NX)
    def _(d):
        pp = (p + d) % NX
        rows = pl.ds(pl.multiple_of(pp * A, A), A)
        send(mbuf.at[rows, :], mfull.at[:, p_cols], ms.at[d], mr.at[p], along_x(pp))

    mfull[:, p_cols] = mbuf[p_rows, :]

    def spread(which, src, i):
        @pl.when(i != j)
        def _():
            send(src, part.at[which, j], ps.at[which, i], pr.at[which, j], plane(i))

        @pl.when(i == j)
        def _():
            part[which, j] = src[...]

    for q in range(G):
        total = dbuf[q, p_rows, :]
        for d in range(1, NX):
            pp = (p + d) % NX
            wait_for(drecv.at[pp, q], dr.at[q, pp])
            total = total + drecv[pp, q]
        for n in range(GC):
            i = q * GC + n
            dsum[i] = total[:, n * L : (n + 1) * L]
            spread(1, dsum.at[i], i)

    @pl.loop(1, NX)
    def _(d):
        pp = (p + d) % NX
        wait_for(mfull.at[:, pl.ds(pl.multiple_of(pp * H, H), H)], mr.at[pp])

    @pl.loop(0, NP)
    def _(i):
        spread(0, mfull.at[:, pl.ds(pl.multiple_of(i * L, L), L)], i)

    @pl.loop(1, NP)
    def _(d):
        i = (j + d) % NP
        wait_for(part.at[1, i], pr.at[1, i])
        wait_for(part.at[0, i], pr.at[0, i])

    acc[NB] = jnp.zeros((A, L), F32)

    @pl.loop(0, NB)
    def _(k):
        total = jnp.zeros((A, L), F32)
        for i in range(NP):
            total = total + jnp.where(tab[0, i] == k, part[0, i], 0.0)
            total = total + jnp.where(tab[1, i] == k, part[1, i], 0.0)
        acc[k] = total

    def first_of(zz):
        return (CP * zz + (j + (NP - CP % NP) * zz) % NP - j) // NP

    @pl.loop(1, NZ)
    def _(d):
        zz = (z + d) % NZ
        send(acc.at[pl.ds(first_of(zz), 2)], q_in.at[z], qs.at[d], qr.at[z], along_z(zz))

    f_own[...] = acc[pl.ds(first_of(z), 2)]

    @pl.loop(1, NZ)
    def _(d):
        zz = (z + NZ - d) % NZ
        wait_for(q_in.at[zz], qr.at[zz])
        f_own[...] += q_in[zz]

    for e in range(2):
        h = hp + NP * e
        i_lo = (L * h) // W
        i_hi = (L * h + L - 1) // W
        for n, i, live in ((0, i_lo, h < CP), (1, i_hi, (h < CP) & (i_hi != i_lo))):
            s = h - (W * i) // L

            @pl.when(live & (i == j))
            def _():
                o_in[s] = f_own[e]

            @pl.when(live & (i != j))
            def _():
                send(f_own.at[e], o_in.at[s], os_.at[e, n], or_.at[s], plane(i))

    for s in range(3):
        h = h0 + s
        holder = (CP * z + h) % NP

        @pl.when((L * h < W * (j + 1)) & (holder != j))
        def _():
            wait_for(o_in.at[s], or_.at[s])

        out_ref[:, s * L : (s + 1) * L] = o_in[s]

    for s in range(3):
        h = h0 + s

        @pl.when((L * h < W * (j + 1)) & ((CP * z + h) % NP != j))
        def _():
            wait_for(img.at[s], s1s.at[s])

    @pl.loop(1, NZ)
    def _(d):
        wait_for(own, s2s.at[d])
        wait_for(acc.at[pl.ds(0, 2)], qs.at[d])

    @pl.loop(1, NP)
    def _(d):
        i = (j + d) % NP
        for which in range(2):
            wait_for(s3s.at[which, d], s3sa.at[which, d])
            wait_for(dsum.at[d], ps.at[which, i])

    @pl.loop(1, NX)
    def _(d):
        wait_for(aop.at[p_rows, :], s4as.at[d])
        wait_for(mbuf.at[p_rows, :], ms.at[d])
        for q in range(G):
            wait_for(bop.at[p_rows, pl.ds(q * GL, GL)], s4bs.at[q, d])
            wait_for(dbuf.at[q, p_rows, :], ds.at[q, d])

    for e in range(2):
        h = hp + NP * e
        i_lo = (L * h) // W
        i_hi = (L * h + L - 1) // W
        for n, i, live in ((0, i_lo, h < CP), (1, i_hi, (h < CP) & (i_hi != i_lo))):

            @pl.when(live & (i != j))
            def _():
                wait_for(f_own.at[e], os_.at[e, n])


def body(n_tile, n_panel, reconstructor, c_as, tiles, tile_pairs, tile_slot):
    A, W = reconstructor.shape
    TS = tiles.shape[2]
    NX = n_panel
    NP = TS // L
    NZ = n_tile // NP
    NB = n_tile * W // TS
    T = tile_slot.shape[0]
    H = TS // NX
    G = NX
    GL = TS // G
    V = pltpu.VMEM
    D = pltpu.SemaphoreType.DMA
    cfg = (A, W, NX, NZ, NP, NB, T)
    chunks = pl.pallas_call(
        functools.partial(kernel, cfg),
        out_shape=jax.ShapeDtypeStruct((A, 3 * L), F32),
        in_specs=[
            pl.BlockSpec(memory_space=pltpu.SMEM),
            pl.BlockSpec(memory_space=pltpu.SMEM),
            pl.BlockSpec(memory_space=pltpu.VMEM),
            pl.BlockSpec(memory_space=pl.ANY),
        ],
        out_specs=pl.BlockSpec(memory_space=pltpu.VMEM),
        scratch_shapes=[
            V((H, TS), BF16),
            V((3, A, L), BF16),
            V((2, 2, A, L), BF16),
            V((2, A, L), BF16),
            V((2 * NZ, A, L), BF16),
            V((2, NP, A, L), BF16),
            V((A, TS), BF16),
            V((A * NX, H), BF16),
            V((A * NX, TS), BF16),
            V((G, A * NX, GL), F32),
            V((A * NX, H), F32),
            V((NX, G, A, GL), F32),
            V((NP, A, L), F32),
            V((A, TS), F32),
            V((2, NP, A, L), F32),
            V((NB + 1, A, L), F32),
            V((NZ, 2, A, L), F32),
            V((2, A, L), F32),
            V((3, A, L), F32),
            pltpu.SMEM((2, NP), jnp.int32),
            D(()),
            D((3,)), D((2, 2)),
            D((NZ,)), D((NZ,)),
            D((2, NP)), D((2, NP)),
            D((NX,)), D((NX,)),
            D((G, NX)), D((G, NX)),
            D((G, NX)), D((G, NX)),
            D((NX,)), D((NX,)),
            D((2, NP)), D((2, NP)),
            D((NZ,)), D((NZ,)),
            D((2, 2)), D((3,)),
        ],
        compiler_params=pltpu.CompilerParams(
            collective_id=0, has_side_effects=True, vmem_limit_bytes=60 * 1024 * 1024
        ),
    )(tile_pairs.T, tile_slot, reconstructor, tiles)
    off = (W * (lax.axis_index("tile") % NP)) % L
    product = lax.dynamic_slice(chunks, (jnp.int32(0), off.astype(jnp.int32)), (A, W))
    return 2.0 * (product - c_as.astype(F32))


def solution(mesh):
    return jax.shard_map(
        functools.partial(body, mesh.shape["tile"], mesh.shape["panel"]),
        mesh=mesh,
        in_specs=(P("panel", "tile"), P("panel", "tile"), P("tile", "panel", None), P(), P()),
        out_specs=P("panel", "tile"),
        check_vma=False,
    )
```

```python
import functools

import jax
import jax.numpy as jnp
from jax import lax
from jax.experimental import pallas as pl
from jax.experimental.pallas import tpu as pltpu
from jax.sharding import PartitionSpec as P

MESH = pl.DeviceIdType.MESH
L = 128
F32 = jnp.float32
BF16 = jnp.bfloat16
I16 = jnp.int16


def wait_for(ref, sem):
    pltpu.make_async_copy(ref, ref, sem).wait()


def code(v):
    top = jnp.maximum(jnp.max(jnp.abs(v), axis=-2, keepdims=True), 1e-30)
    return jnp.round(v * (32767.0 / top)).astype(jnp.int32).astype(jnp.int16), top * (1.0 / 32767.0)


def value(codes, scale):
    return codes.astype(jnp.int32).astype(F32) * scale


def kernel(
    cfg,
    pairs_ref, slot_ref, r_ref, x_hbm,
    out_ref,
    xv, img, c_in, own, gath, s3s, afull, aop, bop, d_own, d_c, d_s, m_c, m_s, d_in, d_in_s, sum_c, sum_s,
    m_in, m_in_s, part, part_s, part_f, acc, acc_c, acc_s, q_in, q_in_s, f_own, o_in, tab,
    x_sem, s1s, s1r, s2s, s2r, s3as, s3ar, s3bs, s3br, s4as, s4ar, s4bs, s4br,
    ds, dr, ms, mr, ps, pr, qs, qr, os_, or_,
):
    A, W, NX, NZ, NP, NB, T = cfg
    TS = NP * L
    H = TS // NX
    CP = NP * W // L
    G = NX
    GL = TS // G
    GC = NP // G
    t = lax.axis_index("tile")
    p = lax.axis_index("panel")
    z = t // NP
    j = t % NP

    def plane(i):
        return {"tile": z * NP + i}

    def along_z(zz):
        return {"tile": zz * NP + j}

    def along_x(pp):
        return {"panel": pp}

    def near_first(n):
        m = NP - 2 - n
        return NP // 2 + (m + 1) // 2 * (2 * (m % 2) - 1)

    def send(src, dst, ssem, rsem, dev):
        pltpu.make_async_remote_copy(
            src_ref=src, dst_ref=dst, send_sem=ssem, recv_sem=rsem, device_id=dev, device_id_type=MESH
        ).start()

    x_copy = pltpu.make_async_copy(x_hbm.at[0], xv, x_sem)
    x_copy.start()

    c_in[...] = jnp.zeros_like(c_in)
    o_in[...] = jnp.zeros_like(o_in)
    h0 = (W * j) // L
    off = W * j - L * h0
    row = lax.broadcasted_iota(jnp.int32, (W, 3 * L), 0)
    col = lax.broadcasted_iota(jnp.int32, (W, 3 * L), 1)
    shift = jnp.where(col - row == off, 1.0, 0.0).astype(BF16)
    placed = jnp.dot(r_ref[...], shift, preferred_element_type=F32).astype(BF16)
    for s in range(3):
        img[s] = placed[:, s * L : (s + 1) * L]

    barrier = pltpu.get_barrier_semaphore()

    @pl.loop(1, NP)
    def _(d):
        pl.semaphore_signal(barrier, inc=1, device_id=plane((j + d) % NP), device_id_type=MESH)

    @pl.loop(1, NZ)
    def _(d):
        pl.semaphore_signal(barrier, inc=1, device_id=along_z((z + d) % NZ), device_id_type=MESH)

    @pl.loop(1, NX)
    def _(d):
        pl.semaphore_signal(barrier, inc=1, device_id=along_x((p + d) % NX), device_id_type=MESH)

    pl.semaphore_wait(barrier, NP + NZ + NX - 3)

    for s in range(3):
        h = h0 + s
        live = L * h < W * (j + 1)
        dest = (CP * z + h) % NP
        e = h // NP
        c = jnp.where((off > 0) & (s == 0), 1, 0)

        @pl.when(live & (dest == j))
        def _():
            c_in[e, c] = img[s]

        @pl.when(live & (dest != j))
        def _():
            send(img.at[s], c_in.at[e, c], s1s.at[s], s1r.at[e, c], plane(dest))

    def look(n, got):
        slot = slot_ref[n]
        code = pairs_ref[0, n] * 16 + pairs_ref[1, n]
        return tuple(jnp.where(slot == z * NP + i, code, got[i]) for i in range(NP))

    found = lax.fori_loop(0, T, look, tuple(jnp.int32(-1) for _ in range(NP)))
    mine = jnp.int32(-1)
    for i in range(NP):
        known = jnp.maximum(found[i], 0)
        tab[0, i] = known // 16
        tab[1, i] = known % 16
        mine = jnp.where(j == i, found[i], mine)
    diag = jnp.where(mine // 16 == mine % 16, 0.5, 1.0)
    factor = jnp.where(mine < 0, 0.0, diag).astype(F32)

    hp = (j + (NP - CP % NP) * z) % NP
    for e in range(2):
        h = hp + NP * e
        i_lo = (L * h) // W
        i_hi = (L * h + L - 1) // W

        @pl.when((h < CP) & (i_lo != j))
        def _():
            wait_for(c_in.at[e, 0], s1r.at[e, 0])

        @pl.when((h < CP) & (i_hi != i_lo) & (i_hi != j))
        def _():
            wait_for(c_in.at[e, 1], s1r.at[e, 1])

        mix = (c_in[e, 0].astype(F32) + c_in[e, 1].astype(F32)).astype(BF16)
        own[e] = mix
        gath[2 * z + e] = mix

    @pl.loop(1, NZ)
    def _(d):
        zz = (z + d) % NZ
        send(own, gath.at[pl.ds(2 * z, 2)], s2s.at[d], s2r.at[z], along_z(zz))

    @pl.loop(1, NZ)
    def _(d):
        zz = (z + NZ - d) % NZ
        wait_for(gath.at[pl.ds(2 * zz, 2)], s2r.at[zz])

    def chunk_of(which, i):
        g = tab[which, i] * NP + j
        return gath[2 * (g // CP) + (g % CP) // NP]

    def plane_stage(which, full, ssem, rsem):
        @pl.loop(0, NP - 1)
        def _(n):
            i = (j + near_first(n)) % NP
            s3s[which, i] = chunk_of(which, i)
            send(s3s.at[which, i], full(j), ssem.at[i], rsem.at[j], plane(i))

    def b_chunk(i):
        return bop.at[i, p]

    def a_chunk(i):
        return afull.at[i]

    plane_stage(1, b_chunk, s3bs, s3br)
    bop[j, p] = chunk_of(1, j)
    plane_stage(0, a_chunk, s3as, s3ar)
    afull[j] = chunk_of(0, j)

    def forward(i):
        @pl.loop(1, NX)
        def _(d):
            send(bop.at[i, p], bop.at[i, p], s4bs.at[i, d], s4br.at[i, p], along_x((p + d) % NX))

    forward(j)

    @pl.loop(0, NP - 1)
    def _(n):
        i = (j + NP - near_first(n)) % NP
        wait_for(bop.at[i, p], s3br.at[i])
        forward(i)

    @pl.loop(1, NP)
    def _(d):
        i = (j + d) % NP
        wait_for(afull.at[i], s3ar.at[i])

    @pl.loop(1, NX)
    def _(d):
        pp = (p + d) % NX
        send(afull.at[pl.ds(pp * GC, GC)], aop.at[p], s4as.at[d], s4ar.at[p], along_x(pp))

    aop[p] = afull[pl.ds(p * GC, GC)]

    @pl.loop(1, NX)
    def _(d):
        pp = (p + d) % NX
        wait_for(aop.at[pp], s4ar.at[pp])

    x_copy.wait()

    def side_by_side(pieces):
        return jnp.concatenate(pieces, axis=1)

    a_rows = jnp.concatenate([side_by_side([aop[pp, n] for n in range(GC)]) for pp in range(NX)], axis=0)

    @pl.loop(0, G)
    def _(q):
        lanes = pl.ds(pl.multiple_of(q * GL, GL), GL)
        prod = jnp.dot(a_rows, xv[:, lanes], preferred_element_type=F32) * factor
        for pp in range(NX):
            for n in range(GC):
                v = prod[pp * A : (pp + 1) * A, n * L : (n + 1) * L]
                d_c[q, pp, n], d_s[q, pp, n] = code(v)

                @pl.when(p == pp)
                def _():
                    d_own[q, n] = v

        @pl.loop(1, NX)
        def _(d):
            pp = (p + d) % NX
            send(d_c.at[q, pp], d_in.at[p, q], ds.at[0, q, d], dr.at[0, q, p], along_x(pp))
            send(d_s.at[q, pp], d_in_s.at[p, q], ds.at[1, q, d], dr.at[1, q, p], along_x(pp))

    prod = jnp.zeros((A * NX, H), F32)
    for q in range(G):

        @pl.loop(1, NX)
        def _(d):
            pp = (p + d) % NX

            @pl.loop(0, GC)
            def _(n):
                wait_for(bop.at[q * GC + n, pp], s4br.at[q * GC + n, pp])

        b_cols = side_by_side([bop[q * GC + n].reshape(NX * A, L) for n in range(GC)])
        prod = prod + lax.dot_general(
            b_cols, xv[:, q * GL : (q + 1) * GL], (((1,), (1,)), ((), ())), preferred_element_type=F32
        )
    prod = prod * factor
    for pp in range(NX):
        for n in range(GC):
            m_c[pp, n], m_s[pp, n] = code(prod[pp * A : (pp + 1) * A, n * L : (n + 1) * L])

    own_chunks = pl.ds(p * GC, GC)

    @pl.loop(1, NX)
    def _(d):
        pp = (p + d) % NX
        send(m_c.at[pp], m_in.at[own_chunks], ms.at[0, d], mr.at[0, p], along_x(pp))
        send(m_s.at[pp], m_in_s.at[own_chunks], ms.at[1, d], mr.at[1, p], along_x(pp))

    m_in[own_chunks] = m_c[p]
    m_in_s[own_chunks] = m_s[p]

    def spread(which, codes, scales, i):
        @pl.when(i != j)
        def _():
            send(codes.at[i], part.at[which, j], ps.at[0, which, i], pr.at[0, which, j], plane(i))
            send(scales.at[i], part_s.at[which, j], ps.at[1, which, i], pr.at[1, which, j], plane(i))

        @pl.when(i == j)
        def _():
            part[which, j] = codes[i]
            part_s[which, j] = scales[i]

    @pl.loop(0, G)
    def _(q):
        @pl.loop(1, NX)
        def _(d):
            pp = (p + d) % NX
            wait_for(d_in.at[pp, q], dr.at[0, q, pp])
            wait_for(d_in_s.at[pp, q], dr.at[1, q, pp])

        @pl.loop(0, GC)
        def _(n):
            total = d_own[q, n]
            for d in range(1, NX):
                pp = (p + d) % NX
                total = total + value(d_in[pp, q, n], d_in_s[pp, q, n])
            i = q * GC + n
            sum_c[i], sum_s[i] = code(total)
            spread(1, sum_c, sum_s, i)

    @pl.loop(1, NX)
    def _(d):
        pp = (p + d) % NX
        wait_for(m_in.at[pl.ds(pp * GC, GC)], mr.at[0, pp])
        wait_for(m_in_s.at[pl.ds(pp * GC, GC)], mr.at[1, pp])

    @pl.loop(0, NP)
    def _(i):
        spread(0, m_in, m_in_s, i)

    for which in (1, 0):
        part_f[which, j] = value(part[which, j], part_s[which, j])

        @pl.loop(1, NP)
        def _(d):
            i = (j + d) % NP
            wait_for(part.at[which, i], pr.at[0, which, i])
            wait_for(part_s.at[which, i], pr.at[1, which, i])
            part_f[which, i] = value(part[which, i], part_s[which, i])

    acc[NB] = jnp.zeros((A, L), F32)
    acc_c[NB], acc_s[NB] = code(acc[NB])

    @pl.loop(0, NB)
    def _(k):
        total = jnp.zeros((A, L), F32)
        for i in range(NP):
            total = total + jnp.where(tab[0, i] == k, part_f[0, i], 0.0)
            total = total + jnp.where(tab[1, i] == k, part_f[1, i], 0.0)
        acc[k] = total
        acc_c[k], acc_s[k] = code(total)

    def first_of(zz):
        return (CP * zz + (j + (NP - CP % NP) * zz) % NP - j) // NP

    @pl.loop(1, NZ)
    def _(d):
        zz = (z + d) % NZ
        two = pl.ds(first_of(zz), 2)
        send(acc_c.at[two], q_in.at[z], qs.at[0, d], qr.at[0, z], along_z(zz))
        send(acc_s.at[two], q_in_s.at[z], qs.at[1, d], qr.at[1, z], along_z(zz))

    f_own[...] = acc[pl.ds(first_of(z), 2)]

    @pl.loop(1, NZ)
    def _(d):
        zz = (z + NZ - d) % NZ
        wait_for(q_in.at[zz], qr.at[0, zz])
        wait_for(q_in_s.at[zz], qr.at[1, zz])
        f_own[...] += value(q_in[zz], q_in_s[zz])

    for e in range(2):
        h = hp + NP * e
        i_lo = (L * h) // W
        i_hi = (L * h + L - 1) // W
        for n, i, live in ((0, i_lo, h < CP), (1, i_hi, (h < CP) & (i_hi != i_lo))):
            s = h - (W * i) // L

            @pl.when(live & (i == j))
            def _():
                o_in[s] = f_own[e]

            @pl.when(live & (i != j))
            def _():
                send(f_own.at[e], o_in.at[s], os_.at[e, n], or_.at[s], plane(i))

    for s in range(3):
        h = h0 + s
        holder = (CP * z + h) % NP

        @pl.when((L * h < W * (j + 1)) & (holder != j))
        def _():
            wait_for(o_in.at[s], or_.at[s])

        out_ref[:, s * L : (s + 1) * L] = o_in[s]

    for s in range(3):
        h = h0 + s

        @pl.when((L * h < W * (j + 1)) & ((CP * z + h) % NP != j))
        def _():
            wait_for(img.at[s], s1s.at[s])

    @pl.loop(1, NZ)
    def _(d):
        wait_for(own, s2s.at[d])
        wait_for(q_in.at[0], qs.at[0, d])
        wait_for(q_in_s.at[0], qs.at[1, d])

    @pl.loop(0, NP)
    def _(i):
        @pl.when(i != j)
        def _():
            wait_for(s3s.at[0, i], s3as.at[i])
            wait_for(s3s.at[1, i], s3bs.at[i])
            for which in range(2):
                wait_for(part.at[which, i], ps.at[0, which, i])
                wait_for(part_s.at[which, i], ps.at[1, which, i])

        @pl.loop(1, NX)
        def _(d):
            wait_for(bop.at[i, p], s4bs.at[i, d])

    @pl.loop(1, NX)
    def _(d):
        wait_for(aop.at[p], s4as.at[d])
        wait_for(m_c.at[p], ms.at[0, d])
        wait_for(m_s.at[p], ms.at[1, d])

        @pl.loop(0, G)
        def _(q):
            wait_for(d_c.at[q, p], ds.at[0, q, d])
            wait_for(d_s.at[q, p], ds.at[1, q, d])

    for e in range(2):
        h = hp + NP * e
        i_lo = (L * h) // W
        i_hi = (L * h + L - 1) // W
        for n, i, live in ((0, i_lo, h < CP), (1, i_hi, (h < CP) & (i_hi != i_lo))):

            @pl.when(live & (i != j))
            def _():
                wait_for(f_own.at[e], os_.at[e, n])


def body(n_tile, n_panel, reconstructor, c_as, tiles, tile_pairs, tile_slot):
    A, W = reconstructor.shape
    TS = tiles.shape[2]
    NX = n_panel
    NP = TS // L
    NZ = n_tile // NP
    NB = n_tile * W // TS
    T = tile_slot.shape[0]
    H = TS // NX
    G = NX
    GC = NP // G
    V = pltpu.VMEM
    D = pltpu.SemaphoreType.DMA
    cfg = (A, W, NX, NZ, NP, NB, T)
    chunks = pl.pallas_call(
        functools.partial(kernel, cfg),
        out_shape=jax.ShapeDtypeStruct((A, 3 * L), F32),
        in_specs=[
            pl.BlockSpec(memory_space=pltpu.SMEM),
            pl.BlockSpec(memory_space=pltpu.SMEM),
            pl.BlockSpec(memory_space=pltpu.VMEM),
            pl.BlockSpec(memory_space=pl.ANY),
        ],
        out_specs=pl.BlockSpec(memory_space=pltpu.VMEM),
        scratch_shapes=[
            V((H, TS), BF16),
            V((3, A, L), BF16),
            V((2, 2, A, L), BF16),
            V((2, A, L), BF16),
            V((2 * NZ, A, L), BF16),
            V((2, NP, A, L), BF16),
            V((NP, A, L), BF16),
            V((NX, GC, A, L), BF16),
            V((NP, NX, A, L), BF16),
            V((G, GC, A, L), F32),
            V((G, NX, GC, A, L), I16), V((G, NX, GC, 1, L), F32),
            V((NX, GC, A, L), I16), V((NX, GC, 1, L), F32),
            V((NX, G, GC, A, L), I16), V((NX, G, GC, 1, L), F32),
            V((NP, A, L), I16), V((NP, 1, L), F32),
            V((NP, A, L), I16), V((NP, 1, L), F32),
            V((2, NP, A, L), I16), V((2, NP, 1, L), F32),
            V((2, NP, A, L), F32),
            V((NB + 1, A, L), F32),
            V((NB + 1, A, L), I16), V((NB + 1, 1, L), F32),
            V((NZ, 2, A, L), I16), V((NZ, 2, 1, L), F32),
            V((2, A, L), F32),
            V((3, A, L), F32),
            pltpu.SMEM((2, NP), jnp.int32),
            D(()),
            D((3,)), D((2, 2)),
            D((NZ,)), D((NZ,)),
            D((NP,)), D((NP,)),
            D((NP,)), D((NP,)),
            D((NX,)), D((NX,)),
            D((NP, NX)), D((NP, NX)),
            D((2, G, NX)), D((2, G, NX)),
            D((2, NX)), D((2, NX)),
            D((2, 2, NP)), D((2, 2, NP)),
            D((2, NZ)), D((2, NZ)),
            D((2, 2)), D((3,)),
        ],
        compiler_params=pltpu.CompilerParams(
            collective_id=0, has_side_effects=True, vmem_limit_bytes=60 * 1024 * 1024
        ),
    )(tile_pairs.T, tile_slot, reconstructor, tiles)
    off = (W * (lax.axis_index("tile") % NP)) % L
    product = lax.dynamic_slice(chunks, (jnp.int32(0), off.astype(jnp.int32)), (A, W))
    return 2.0 * (product - c_as.astype(F32))


def solution(mesh):
    return jax.shard_map(
        functools.partial(body, mesh.shape["tile"], mesh.shape["panel"]),
        mesh=mesh,
        in_specs=(P("panel", "tile"), P("panel", "tile"), P("tile", "panel", None), P(), P()),
        out_specs=P("panel", "tile"),
        check_vma=False,
    )
```

```python
import functools

import jax
import jax.numpy as jnp
from jax import lax
from jax.experimental import pallas as pl
from jax.experimental.pallas import tpu as pltpu
from jax.sharding import PartitionSpec as P

MESH = pl.DeviceIdType.MESH
L = 128
F32 = jnp.float32
BF16 = jnp.bfloat16
I16 = jnp.int16


def wait_for(ref, sem):
    pltpu.make_async_copy(ref, ref, sem).wait()


def div(x, n):
    return lax.div(x, jnp.int32(n))


def rem(x, n):
    return lax.rem(x, jnp.int32(n))


def code(v):
    top = jnp.maximum(jnp.max(jnp.abs(v), axis=-2, keepdims=True), 1e-30)
    return jnp.round(v * (32767.0 / top)).astype(jnp.int32).astype(jnp.int16), top * (1.0 / 32767.0)


def value(codes, scale):
    return codes.astype(jnp.int32).astype(F32) * scale


def kernel(
    cfg,
    pairs_ref, slot_ref, r_ref, x_hbm,
    out_ref,
    xv, img, c_in, own, gath, s3s, afull, a_in_order, aop, bop, d_own, d_c, d_s, m_c, m_s, d_in, d_in_s, sum_c, sum_s,
    m_in, m_in_s, m_out, m_out_s, part, part_s, part_f, acc, acc_c, acc_s, q_in, q_in_s, f_own, o_in, tab, place,
    x_sem, s1s, s1r, s2s, s2r, s3as, s3ar, s3bs, s3br, s4as, s4ar, s4bs, s4br,
    ds, dr, ms, mr, ps, pr, qs, qr, os_, or_,
):
    A, W, NX, NZ, NP, NB, T = cfg
    TS = NP * L
    H = TS // NX
    CP = NP * W // L
    G = NX
    GC = NP // G
    t = lax.axis_index("tile")
    p = lax.axis_index("panel")
    z = t // NP
    j = t % NP

    def plane(i):
        return {"tile": z * NP + i}

    def along_z(zz):
        return {"tile": zz * NP + j}

    def along_x(pp):
        return {"panel": pp}

    def far_first(n):
        return NP // 2 + (n + 1) // 2 * (2 * (n % 2) - 1)

    def near_first(n):
        return far_first(NP - 2 - n)


    def send(src, dst, ssem, rsem, dev):
        pltpu.make_async_remote_copy(
            src_ref=src, dst_ref=dst, send_sem=ssem, recv_sem=rsem, device_id=dev, device_id_type=MESH
        ).start()

    SH = (NP * (W - L) // W) // 2
    BIG = NP * (1 + L * NB // W)

    def chunk_no(k, pos):
        return NP * k + rem(pos + SH + BIG - div(L * NP * k, W), NP)

    def slot_of(k, pos):
        zz = div(chunk_no(k, pos), CP)
        return zz, jnp.where((k > 0) & (chunk_no(k - 1, pos) >= CP * zz), 1, 0)

    def first_of(zz):
        k = div(CP * zz, NP)
        return k + jnp.where(chunk_no(k, j) < CP * zz, 1, 0)

    for i in range(NP):
        pltpu.make_async_copy(x_hbm.at[0, :, pl.ds(i * L, L)], xv.at[i], x_sem).start()

    c_in[...] = jnp.zeros_like(c_in)
    o_in[...] = jnp.zeros_like(o_in)
    barrier = pltpu.get_barrier_semaphore()

    @pl.loop(1, NP)
    def _(d):
        pl.semaphore_signal(barrier, inc=1, device_id=plane((j + d) % NP), device_id_type=MESH)

    @pl.loop(1, NZ)
    def _(d):
        pl.semaphore_signal(barrier, inc=1, device_id=along_z((z + d) % NZ), device_id_type=MESH)

    @pl.loop(1, NX)
    def _(d):
        pl.semaphore_signal(barrier, inc=1, device_id=along_x((p + d) % NX), device_id_type=MESH)

    h0 = (W * j) // L
    off = W * j - L * h0
    row = lax.broadcasted_iota(jnp.int32, (W, 3 * L), 0)
    col = lax.broadcasted_iota(jnp.int32, (W, 3 * L), 1)
    shift = jnp.where(col - row == off, 1.0, 0.0).astype(BF16)
    placed = jnp.dot(r_ref[...], shift, preferred_element_type=F32).astype(BF16)
    for s in range(3):
        img[s] = placed[:, s * L : (s + 1) * L]

    pl.semaphore_wait(barrier, NP + NZ + NX - 3)

    for s in range(3):
        h = h0 + s
        live = L * h < W * (j + 1)
        block, rest = div(CP * z + h, NP), rem(CP * z + h, NP)
        dest = rem(rest + div(L * NP * block, W) + NP - SH, NP)
        _, e = slot_of(block, dest)
        c = jnp.where((off > 0) & (s == 0), 1, 0)

        @pl.when(live & (dest == j))
        def _():
            c_in[e, c] = img[s]

        @pl.when(live & (dest != j))
        def _():
            send(img.at[s], c_in.at[e, c], s1s.at[s], s1r.at[e, c], plane(dest))

    def look(n, got):
        slot = slot_ref[n]
        code = pairs_ref[0, n] * 16 + pairs_ref[1, n]
        return tuple(jnp.where(slot == z * NP + i, code, got[i]) for i in range(NP))

    found = lax.fori_loop(0, T, look, tuple(jnp.int32(-1) for _ in range(NP)))
    mine = jnp.int32(-1)
    for i in range(NP):
        known = jnp.maximum(found[i], 0)
        for which, block in enumerate((known // 16, known % 16)):
            tab[which, i] = block
            zz, e = slot_of(block, j)
            place[which, i] = 2 * zz + e
        mine = jnp.where(j == i, found[i], mine)
    known = jnp.maximum(mine, 0)
    turn_a = rem(div(L * NP * (known // 16), W) + NP - SH, NP)
    turn_b = rem(div(L * NP * (known % 16), W) + NP - SH, NP)
    diag = jnp.where(mine // 16 == mine % 16, 0.5, 1.0)
    factor = jnp.where(mine < 0, 0.0, diag).astype(F32)

    mine_first = first_of(z)

    def chunk_at(e):
        h = chunk_no(mine_first + e, j) - CP * z
        return h, (mine_first + e < NB) & (h < CP)

    for e in range(2):
        h, live = chunk_at(e)
        i_lo = (L * h) // W
        i_hi = (L * h + L - 1) // W

        @pl.when(live & (i_lo != j))
        def _():
            wait_for(c_in.at[e, 0], s1r.at[e, 0])

        @pl.when(live & (i_hi != i_lo) & (i_hi != j))
        def _():
            wait_for(c_in.at[e, 1], s1r.at[e, 1])

        mix = (c_in[e, 0].astype(F32) + c_in[e, 1].astype(F32)).astype(BF16)
        own[e] = mix
        gath[2 * z + e] = mix

    @pl.loop(1, NZ)
    def _(n):
        d = NZ // 2 + n // 2 * (2 * ((n - 1) % 2) - 1)
        zz = (z + d) % NZ
        send(own, gath.at[pl.ds(2 * z, 2)], s2s.at[d], s2r.at[z], along_z(zz))

    @pl.loop(1, NZ)
    def _(d):
        zz = (z + NZ - d) % NZ
        wait_for(gath.at[pl.ds(2 * zz, 2)], s2r.at[zz])

    def chunk_of(which, i):
        return gath[place[which, i]]

    def plane_stage(which, full, ssem, rsem):
        @pl.loop(0, NP - 1)
        def _(n):
            i = (j + near_first(n)) % NP
            s3s[which, i] = chunk_of(which, i)
            send(s3s.at[which, i], full(j), ssem.at[i], rsem.at[j], plane(i))

    def b_chunk(i):
        return bop.at[i, p]

    def a_chunk(i):
        return afull.at[i]

    plane_stage(1, b_chunk, s3bs, s3br)
    bop[j, p] = chunk_of(1, j)
    plane_stage(0, a_chunk, s3as, s3ar)
    afull[j] = chunk_of(0, j)

    def forward(i):
        @pl.loop(1, NX)
        def _(d):
            send(bop.at[i, p], bop.at[i, p], s4bs.at[i, d], s4br.at[i, p], along_x((p + d) % NX))

    forward(j)

    @pl.loop(0, NP - 1)
    def _(n):
        i = (j + NP - near_first(n)) % NP
        wait_for(bop.at[i, p], s3br.at[i])
        forward(i)

    wait_for(xv, x_sem)

    def x_chunk(i):
        return xv[rem(i + NP - turn_b, NP)]

    def side_by_side(pieces):
        return jnp.concatenate(pieces, axis=1)

    @pl.loop(1, NP)
    def _(d):
        i = (j + d) % NP
        wait_for(afull.at[i], s3ar.at[i])

    for i in range(NP):
        a_in_order[i] = afull[rem(i + turn_a, NP)]

    @pl.loop(1, NX)
    def _(d):
        pp = (p + d) % NX
        send(a_in_order.at[pl.ds(pp * GC, GC)], aop.at[p], s4as.at[d], s4ar.at[p], along_x(pp))

    aop[p] = a_in_order[pl.ds(p * GC, GC)]

    prod = jnp.zeros((A * NX, H), F32)
    for q in range(G):

        @pl.loop(1, NX)
        def _(d):
            pp = (p + d) % NX

            @pl.loop(0, GC)
            def _(n):
                wait_for(bop.at[q * GC + n, pp], s4br.at[q * GC + n, pp])

        b_cols = side_by_side([bop[q * GC + n].reshape(NX * A, L) for n in range(GC)])
        x_cols = side_by_side([x_chunk(q * GC + n) for n in range(GC)])
        prod = prod + lax.dot_general(b_cols, x_cols, (((1,), (1,)), ((), ())), preferred_element_type=F32)
    prod = prod * factor
    for pp in range(NX):
        for n in range(GC):
            m_c[pp, n], m_s[pp, n] = code(prod[pp * A : (pp + 1) * A, n * L : (n + 1) * L])

    own_chunks = pl.ds(p * GC, GC)

    @pl.loop(1, NX)
    def _(d):
        pp = (p + d) % NX
        send(m_c.at[pp], m_in.at[own_chunks], ms.at[0, d], mr.at[0, p], along_x(pp))
        send(m_s.at[pp], m_in_s.at[own_chunks], ms.at[1, d], mr.at[1, p], along_x(pp))

    m_in[own_chunks] = m_c[p]
    m_in_s[own_chunks] = m_s[p]

    @pl.loop(1, NX)
    def _(d):
        pp = (p + d) % NX
        wait_for(aop.at[pp], s4ar.at[pp])

    a_rows = jnp.concatenate([side_by_side([aop[pp, n] for n in range(GC)]) for pp in range(NX)], axis=0)

    def group(n):
        return (n + j // GC) % G

    @pl.loop(0, G)
    def _(step):
        q = group(step)
        x_cols = side_by_side([x_chunk(q * GC + n) for n in range(GC)])
        prod = jnp.dot(a_rows, x_cols, preferred_element_type=F32) * factor
        for pp in range(NX):
            for n in range(GC):
                v = prod[pp * A : (pp + 1) * A, n * L : (n + 1) * L]
                d_c[q, pp, n], d_s[q, pp, n] = code(v)

                @pl.when(p == pp)
                def _():
                    d_own[q, n] = v

        @pl.loop(1, NX)
        def _(d):
            pp = (p + d) % NX
            send(d_c.at[q, pp], d_in.at[p, q], ds.at[0, q, d], dr.at[0, q, p], along_x(pp))
            send(d_s.at[q, pp], d_in_s.at[p, q], ds.at[1, q, d], dr.at[1, q, p], along_x(pp))

    def spread(which, codes, scales, i):
        @pl.when(i != j)
        def _():
            send(codes.at[i], part.at[which, j], ps.at[0, which, i], pr.at[0, which, j], plane(i))
            send(scales.at[i], part_s.at[which, j], ps.at[1, which, i], pr.at[1, which, j], plane(i))

        @pl.when(i == j)
        def _():
            part[which, j] = codes[i]
            part_s[which, j] = scales[i]

    @pl.loop(1, NX)
    def _(d):
        pp = (p + d) % NX
        wait_for(m_in.at[pl.ds(pp * GC, GC)], mr.at[0, pp])
        wait_for(m_in_s.at[pl.ds(pp * GC, GC)], mr.at[1, pp])

    @pl.loop(0, NP)
    def _(n):
        i = (j + far_first(n)) % NP
        r = rem(i + NP - turn_a, NP)
        m_out[i] = m_in[r]
        m_out_s[i] = m_in_s[r]
        spread(0, m_out, m_out_s, i)

    @pl.loop(0, G)
    def _(step):
        q = group(step)

        @pl.loop(1, NX)
        def _(d):
            pp = (p + d) % NX
            wait_for(d_in.at[pp, q], dr.at[0, q, pp])
            wait_for(d_in_s.at[pp, q], dr.at[1, q, pp])

        @pl.loop(0, GC)
        def _(turn):
            n = (turn + j) % GC
            total = d_own[q, n]
            for d in range(1, NX):
                pp = (p + d) % NX
                total = total + value(d_in[pp, q, n], d_in_s[pp, q, n])
            i = q * GC + n
            sum_c[i], sum_s[i] = code(total)
            spread(1, sum_c, sum_s, i)

    for which in (0, 1):

        @pl.loop(1, NP)
        def _(d):
            i = (j + d) % NP
            wait_for(part.at[which, i], pr.at[0, which, i])
            wait_for(part_s.at[which, i], pr.at[1, which, i])

        for i in range(NP):
            part_f[i] = value(part[which, i], part_s[which, i])

        @pl.loop(0, NB)
        def _(k):
            total = acc[k] if which else jnp.zeros((A, L), F32)
            for i in range(NP):
                total = total + jnp.where(tab[which, i] == k, part_f[i], 0.0)
            acc[k] = total
            if which:
                acc_c[k], acc_s[k] = code(total)

    acc_c[NB], acc_s[NB] = code(jnp.zeros((A, L), F32))

    @pl.loop(1, NZ)
    def _(n):
        d = NZ // 2 + n // 2 * (2 * ((n - 1) % 2) - 1)
        zz = (z + d) % NZ
        two = pl.ds(first_of(zz), 2)
        send(acc_c.at[two], q_in.at[z], qs.at[0, d], qr.at[0, z], along_z(zz))
        send(acc_s.at[two], q_in_s.at[z], qs.at[1, d], qr.at[1, z], along_z(zz))

    f_own[0] = acc[mine_first]
    f_own[1] = acc[jnp.minimum(mine_first + 1, NB - 1)]

    @pl.loop(1, NZ)
    def _(d):
        zz = (z + NZ - d) % NZ
        wait_for(q_in.at[zz], qr.at[0, zz])
        wait_for(q_in_s.at[zz], qr.at[1, zz])
        f_own[...] += value(q_in[zz], q_in_s[zz])

    for e in range(2):
        h, here = chunk_at(e)
        i_lo = (L * h) // W
        i_hi = (L * h + L - 1) // W
        for n, i, live in ((0, i_lo, here), (1, i_hi, here & (i_hi != i_lo))):
            s = h - (W * i) // L

            @pl.when(live & (i == j))
            def _():
                o_in[s] = f_own[e]

            @pl.when(live & (i != j))
            def _():
                send(f_own.at[e], o_in.at[s], os_.at[e, n], or_.at[s], plane(i))

    for s in range(3):
        h = h0 + s
        block, rest = div(CP * z + h, NP), rem(CP * z + h, NP)
        holder = rem(rest + div(L * NP * block, W) + NP - SH, NP)

        @pl.when((L * h < W * (j + 1)) & (holder != j))
        def _():
            wait_for(o_in.at[s], or_.at[s])

    wide = side_by_side([o_in[s] for s in range(3)])
    out_ref[...] = pltpu.roll(wide, rem(3 * L - off, 3 * L), 1)[:, :W]

    for s in range(3):
        h = h0 + s

        block, rest = div(CP * z + h, NP), rem(CP * z + h, NP)
        holder = rem(rest + div(L * NP * block, W) + NP - SH, NP)

        @pl.when((L * h < W * (j + 1)) & (holder != j))
        def _():
            wait_for(img.at[s], s1s.at[s])

    @pl.loop(1, NZ)
    def _(d):
        wait_for(own, s2s.at[d])
        wait_for(q_in.at[0], qs.at[0, d])
        wait_for(q_in_s.at[0], qs.at[1, d])

    @pl.loop(0, NP)
    def _(i):
        @pl.when(i != j)
        def _():
            wait_for(s3s.at[0, i], s3as.at[i])
            wait_for(s3s.at[1, i], s3bs.at[i])
            for which in range(2):
                wait_for(part.at[which, i], ps.at[0, which, i])
                wait_for(part_s.at[which, i], ps.at[1, which, i])

        @pl.loop(1, NX)
        def _(d):
            wait_for(bop.at[i, p], s4bs.at[i, d])

    @pl.loop(1, NX)
    def _(d):
        wait_for(aop.at[p], s4as.at[d])
        wait_for(m_c.at[p], ms.at[0, d])
        wait_for(m_s.at[p], ms.at[1, d])

        @pl.loop(0, G)
        def _(q):
            wait_for(d_c.at[q, p], ds.at[0, q, d])
            wait_for(d_s.at[q, p], ds.at[1, q, d])

    for e in range(2):
        h, here = chunk_at(e)
        i_lo = (L * h) // W
        i_hi = (L * h + L - 1) // W
        for n, i, live in ((0, i_lo, here), (1, i_hi, here & (i_hi != i_lo))):

            @pl.when(live & (i != j))
            def _():
                wait_for(f_own.at[e], os_.at[e, n])


def body(n_tile, n_panel, reconstructor, c_as, tiles, tile_pairs, tile_slot):
    A, W = reconstructor.shape
    TS = tiles.shape[2]
    NX = n_panel
    NP = TS // L
    NZ = n_tile // NP
    NB = n_tile * W // TS
    T = tile_slot.shape[0]
    H = TS // NX
    G = NX
    GC = NP // G
    V = pltpu.VMEM
    D = pltpu.SemaphoreType.DMA
    cfg = (A, W, NX, NZ, NP, NB, T)
    product = pl.pallas_call(
        functools.partial(kernel, cfg),
        out_shape=jax.ShapeDtypeStruct((A, W), F32),
        in_specs=[
            pl.BlockSpec(memory_space=pltpu.SMEM),
            pl.BlockSpec(memory_space=pltpu.SMEM),
            pl.BlockSpec(memory_space=pltpu.VMEM),
            pl.BlockSpec(memory_space=pl.ANY),
        ],
        out_specs=pl.BlockSpec(memory_space=pltpu.VMEM),
        scratch_shapes=[
            V((NP, H, L), BF16),
            V((3, A, L), BF16),
            V((2, 2, A, L), BF16),
            V((2, A, L), BF16),
            V((2 * NZ, A, L), BF16),
            V((2, NP, A, L), BF16),
            V((NP, A, L), BF16), V((NP, A, L), BF16),
            V((NX, GC, A, L), BF16),
            V((NP, NX, A, L), BF16),
            V((G, GC, A, L), F32),
            V((G, NX, GC, A, L), I16), V((G, NX, GC, 1, L), F32),
            V((NX, GC, A, L), I16), V((NX, GC, 1, L), F32),
            V((NX, G, GC, A, L), I16), V((NX, G, GC, 1, L), F32),
            V((NP, A, L), I16), V((NP, 1, L), F32),
            V((NP, A, L), I16), V((NP, 1, L), F32),
            V((NP, A, L), I16), V((NP, 1, L), F32),
            V((2, NP, A, L), I16), V((2, NP, 1, L), F32),
            V((NP, A, L), F32),
            V((NB, A, L), F32),
            V((NB + 1, A, L), I16), V((NB + 1, 1, L), F32),
            V((NZ, 2, A, L), I16), V((NZ, 2, 1, L), F32),
            V((2, A, L), F32),
            V((3, A, L), F32),
            pltpu.SMEM((2, NP), jnp.int32), pltpu.SMEM((2, NP), jnp.int32),
            D(()),
            D((3,)), D((2, 2)),
            D((NZ,)), D((NZ,)),
            D((NP,)), D((NP,)),
            D((NP,)), D((NP,)),
            D((NX,)), D((NX,)),
            D((NP, NX)), D((NP, NX)),
            D((2, G, NX)), D((2, G, NX)),
            D((2, NX)), D((2, NX)),
            D((2, 2, NP)), D((2, 2, NP)),
            D((2, NZ)), D((2, NZ)),
            D((2, 2)), D((3,)),
        ],
        compiler_params=pltpu.CompilerParams(
            collective_id=0, has_side_effects=True, vmem_limit_bytes=60 * 1024 * 1024
        ),
    )(tile_pairs.T, tile_slot, reconstructor, tiles)
    return 2.0 * (product - c_as.astype(F32))


def solution(mesh):
    return jax.shard_map(
        functools.partial(body, mesh.shape["tile"], mesh.shape["panel"]),
        mesh=mesh,
        in_specs=(P("panel", "tile"), P("panel", "tile"), P("tile", "panel", None), P(), P()),
        out_specs=P("panel", "tile"),
        check_vma=False,
    )
```

```python
import functools

import jax
import jax.numpy as jnp
from jax import lax
from jax.experimental import pallas as pl
from jax.experimental.pallas import tpu as pltpu
from jax.sharding import PartitionSpec as P

MESH = pl.DeviceIdType.MESH
L = 128
F32 = jnp.float32
BF16 = jnp.bfloat16
I16 = jnp.int16


def wait_for(ref, sem):
    pltpu.make_async_copy(ref, ref, sem).wait()


def div(x, n):
    return lax.div(x, jnp.int32(n))


def rem(x, n):
    return lax.rem(x, jnp.int32(n))


def code(v):
    top = jnp.maximum(jnp.max(jnp.abs(v), axis=-2, keepdims=True), 1e-30)
    return jnp.round(v * (32767.0 / top)).astype(jnp.int32).astype(jnp.int16), top * (1.0 / 32767.0)


def value(codes, scale):
    return codes.astype(jnp.int32).astype(F32) * scale


def kernel(
    cfg,
    pairs_ref, slot_ref, r_ref, x_hbm,
    out_ref,
    xv, wide, img, c_in, own, gath, s3s, afull, a_in_order, aop, bop, d_own, d_c, d_s, m_c, m_s, d_in, d_in_s, sum_c, sum_s,
    m_in, m_in_s, m_out, m_out_s, part, part_s, part_f, acc, acc_c, acc_s, q_in, q_in_s, f_own, o_in, tab, place,
    x_sem, passed_z, passed_plane, s1s, s1r, s2s, s2r, s3as, s3ar, s3bs, s3br, s4as, s4ar, s4bs, s4br,
    ds, dr, ms, mr, ps, pr, qs, qr, os_, or_,
):
    A, W, NX, NZ, NP, NB, T = cfg
    TS = NP * L
    H = TS // NX
    CP = NP * W // L
    G = NX
    GC = NP // G
    t = lax.axis_index("tile")
    p = lax.axis_index("panel")
    z = t // NP
    j = t % NP

    def plane(i):
        return {"tile": z * NP + i}

    def along_z(zz):
        return {"tile": zz * NP + j}

    def along_x(pp):
        return {"panel": pp}

    def far_first(n):
        return NP // 2 + (n + 1) // 2 * (2 * (n % 2) - 1)

    def near_first(n):
        return far_first(NP - 2 - n)


    def send(src, dst, ssem, rsem, dev):
        pltpu.make_async_remote_copy(
            src_ref=src, dst_ref=dst, send_sem=ssem, recv_sem=rsem, device_id=dev, device_id_type=MESH
        ).start()

    SH = (NP * (W - L) // W) // 2
    BIG = NP * (1 + L * NB // W)

    def chunk_no(k, pos):
        return NP * k + rem(pos + SH + BIG - div(L * NP * k, W), NP)

    def slot_of(k, pos):
        zz = div(chunk_no(k, pos), CP)
        return zz, jnp.where((k > 0) & (chunk_no(k - 1, pos) >= CP * zz), 1, 0)

    def first_of(zz):
        k = div(CP * zz, NP)
        return k + jnp.where(chunk_no(k, j) < CP * zz, 1, 0)


    c_in[...] = jnp.zeros_like(c_in)
    o_in[...] = jnp.zeros_like(o_in)
    barrier = pltpu.get_barrier_semaphore()

    REACH = 2
    CHIPS = NP // 2
    near_plane = 2 * min(CHIPS, 2 * REACH + 1) - 1
    near_z = min(NZ, 2 * REACH + 1) - 1

    def tell_plane(sem):
        for away in range(-min(REACH, (CHIPS - 1) // 2), min(REACH, CHIPS // 2) + 1):
            for core in range(2):
                i = 2 * ((j // 2 + away + CHIPS) % CHIPS) + core

                @pl.when(i != j)
                def _():
                    pl.semaphore_signal(sem, inc=1, device_id=plane(i), device_id_type=MESH)

    def tell_z(sem):
        for d in range(1, NZ):
            if min(d, NZ - d) <= REACH:
                pl.semaphore_signal(sem, inc=1, device_id=along_z((z + d) % NZ), device_id_type=MESH)

    tell_plane(barrier)
    tell_z(barrier)

    @pl.loop(1, NX)
    def _(d):
        pl.semaphore_signal(barrier, inc=1, device_id=along_x((p + d) % NX), device_id_type=MESH)

    h0 = (W * j) // L
    off = W * j - L * h0
    wide[...] = jnp.zeros_like(wide)
    wide[:, :W] = r_ref[...].astype(F32)
    placed = pltpu.roll(wide[...], off, 1).astype(BF16)
    for s in range(3):
        img[s] = placed[:, s * L : (s + 1) * L]

    pl.semaphore_wait(barrier, near_plane + near_z + NX - 1)

    for s in range(3):
        h = h0 + s
        live = L * h < W * (j + 1)
        block, rest = div(CP * z + h, NP), rem(CP * z + h, NP)
        dest = rem(rest + div(L * NP * block, W) + NP - SH, NP)
        _, e = slot_of(block, dest)
        c = jnp.where((off > 0) & (s == 0), 1, 0)

        @pl.when(live & (dest == j))
        def _():
            c_in[e, c] = img[s]

        @pl.when(live & (dest != j))
        def _():
            send(img.at[s], c_in.at[e, c], s1s.at[s], s1r.at[e, c], plane(dest))

    tell_z(passed_z)
    tell_plane(passed_plane)

    for i in range(NP):
        pltpu.make_async_copy(x_hbm.at[0, :, pl.ds(i * L, L)], xv.at[i], x_sem).start()

    mine_first = first_of(z)

    def chunk_at(e):
        h = chunk_no(mine_first + e, j) - CP * z
        return h, (mine_first + e < NB) & (h < CP)

    for e in range(2):
        h, live = chunk_at(e)
        i_lo = (L * h) // W
        i_hi = (L * h + L - 1) // W

        @pl.when(live & (i_lo != j))
        def _():
            wait_for(c_in.at[e, 0], s1r.at[e, 0])

        @pl.when(live & (i_hi != i_lo) & (i_hi != j))
        def _():
            wait_for(c_in.at[e, 1], s1r.at[e, 1])

        mix = (c_in[e, 0].astype(F32) + c_in[e, 1].astype(F32)).astype(BF16)
        own[e] = mix
        gath[2 * z + e] = mix

    pl.semaphore_wait(passed_z, near_z)
    @pl.loop(1, NZ)
    def _(n):
        d = NZ // 2 + n // 2 * (2 * ((n - 1) % 2) - 1)
        zz = (z + d) % NZ
        send(own, gath.at[pl.ds(2 * z, 2)], s2s.at[d], s2r.at[z], along_z(zz))

    def look(n, got):
        slot = slot_ref[n]
        code = pairs_ref[0, n] * 16 + pairs_ref[1, n]
        return tuple(jnp.where(slot == z * NP + i, code, got[i]) for i in range(NP))

    found = lax.fori_loop(0, T, look, tuple(jnp.int32(-1) for _ in range(NP)))
    mine = jnp.int32(-1)
    for i in range(NP):
        known = jnp.maximum(found[i], 0)
        for which, block in enumerate((known // 16, known % 16)):
            tab[which, i] = block
            zz, e = slot_of(block, j)
            place[which, i] = 2 * zz + e
        mine = jnp.where(j == i, found[i], mine)
    known = jnp.maximum(mine, 0)
    turn_a = rem(div(L * NP * (known // 16), W) + NP - SH, NP)
    turn_b = rem(div(L * NP * (known % 16), W) + NP - SH, NP)
    diag = jnp.where(mine // 16 == mine % 16, 0.5, 1.0)
    factor = jnp.where(mine < 0, 0.0, diag).astype(F32)

    @pl.loop(1, NZ)
    def _(d):
        zz = (z + NZ - d) % NZ
        wait_for(gath.at[pl.ds(2 * zz, 2)], s2r.at[zz])

    def chunk_of(which, i):
        return gath[place[which, i]]

    pl.semaphore_wait(passed_plane, near_plane)

    def plane_stage(which, full, ssem, rsem):
        @pl.loop(0, NP - 1)
        def _(n):
            i = (j + near_first(n)) % NP
            s3s[which, i] = chunk_of(which, i)
            send(s3s.at[which, i], full(j), ssem.at[i], rsem.at[j], plane(i))

    def b_chunk(i):
        return bop.at[i, p]

    def a_chunk(i):
        return afull.at[i]

    plane_stage(1, b_chunk, s3bs, s3br)
    bop[j, p] = chunk_of(1, j)
    plane_stage(0, a_chunk, s3as, s3ar)
    afull[j] = chunk_of(0, j)

    def forward(i):
        @pl.loop(1, NX)
        def _(d):
            send(bop.at[i, p], bop.at[i, p], s4bs.at[i, d], s4br.at[i, p], along_x((p + d) % NX))

    forward(j)

    @pl.loop(0, NP - 1)
    def _(n):
        i = (j + NP - near_first(n)) % NP
        wait_for(bop.at[i, p], s3br.at[i])
        forward(i)

    wait_for(xv, x_sem)

    def x_chunk(i):
        return xv[rem(i + NP - turn_b, NP)]

    def side_by_side(pieces):
        return jnp.concatenate(pieces, axis=1)

    @pl.loop(1, NP)
    def _(d):
        i = (j + d) % NP
        wait_for(afull.at[i], s3ar.at[i])

    for i in range(NP):
        a_in_order[i] = afull[rem(i + turn_a, NP)]

    @pl.loop(1, NX)
    def _(d):
        pp = (p + d) % NX
        send(a_in_order.at[pl.ds(pp * GC, GC)], aop.at[p], s4as.at[d], s4ar.at[p], along_x(pp))

    aop[p] = a_in_order[pl.ds(p * GC, GC)]

    prod = jnp.zeros((A * NX, H), F32)
    for q in range(G):

        @pl.loop(1, NX)
        def _(d):
            pp = (p + d) % NX

            @pl.loop(0, GC)
            def _(n):
                wait_for(bop.at[q * GC + n, pp], s4br.at[q * GC + n, pp])

        b_cols = side_by_side([bop[q * GC + n].reshape(NX * A, L) for n in range(GC)])
        x_cols = side_by_side([x_chunk(q * GC + n) for n in range(GC)])
        prod = prod + lax.dot_general(b_cols, x_cols, (((1,), (1,)), ((), ())), preferred_element_type=F32)
    prod = prod * factor
    for pp in range(NX):
        for n in range(GC):
            m_c[pp, n], m_s[pp, n] = code(prod[pp * A : (pp + 1) * A, n * L : (n + 1) * L])

    own_chunks = pl.ds(p * GC, GC)

    @pl.loop(1, NX)
    def _(d):
        pp = (p + d) % NX
        send(m_c.at[pp], m_in.at[own_chunks], ms.at[0, d], mr.at[0, p], along_x(pp))
        send(m_s.at[pp], m_in_s.at[own_chunks], ms.at[1, d], mr.at[1, p], along_x(pp))

    m_in[own_chunks] = m_c[p]
    m_in_s[own_chunks] = m_s[p]

    @pl.loop(1, NX)
    def _(d):
        pp = (p + d) % NX
        wait_for(aop.at[pp], s4ar.at[pp])

    a_rows = jnp.concatenate([side_by_side([aop[pp, n] for n in range(GC)]) for pp in range(NX)], axis=0)

    def group(n):
        return (n + j // GC) % G

    @pl.loop(0, G)
    def _(step):
        q = group(step)
        x_cols = side_by_side([x_chunk(q * GC + n) for n in range(GC)])
        prod = jnp.dot(a_rows, x_cols, preferred_element_type=F32) * factor
        for pp in range(NX):
            for n in range(GC):
                v = prod[pp * A : (pp + 1) * A, n * L : (n + 1) * L]
                d_c[q, pp, n], d_s[q, pp, n] = code(v)

                @pl.when(p == pp)
                def _():
                    d_own[q, n] = v

        @pl.loop(1, NX)
        def _(d):
            pp = (p + d) % NX
            send(d_c.at[q, pp], d_in.at[p, q], ds.at[0, q, d], dr.at[0, q, p], along_x(pp))
            send(d_s.at[q, pp], d_in_s.at[p, q], ds.at[1, q, d], dr.at[1, q, p], along_x(pp))

    def spread(which, codes, scales, i):
        @pl.when(i != j)
        def _():
            send(codes.at[i], part.at[which, j], ps.at[0, which, i], pr.at[0, which, j], plane(i))
            send(scales.at[i], part_s.at[which, j], ps.at[1, which, i], pr.at[1, which, j], plane(i))

        @pl.when(i == j)
        def _():
            part[which, j] = codes[i]
            part_s[which, j] = scales[i]

    @pl.loop(1, NX)
    def _(d):
        pp = (p + d) % NX
        wait_for(m_in.at[pl.ds(pp * GC, GC)], mr.at[0, pp])
        wait_for(m_in_s.at[pl.ds(pp * GC, GC)], mr.at[1, pp])

    @pl.loop(0, NP)
    def _(n):
        i = (j + far_first(n)) % NP
        r = rem(i + NP - turn_a, NP)
        m_out[i] = m_in[r]
        m_out_s[i] = m_in_s[r]
        spread(0, m_out, m_out_s, i)

    @pl.loop(0, G)
    def _(step):
        q = group(step)

        @pl.loop(1, NX)
        def _(d):
            pp = (p + d) % NX
            wait_for(d_in.at[pp, q], dr.at[0, q, pp])
            wait_for(d_in_s.at[pp, q], dr.at[1, q, pp])

        @pl.loop(0, GC)
        def _(turn):
            n = (turn + j) % GC
            total = d_own[q, n]
            for d in range(1, NX):
                pp = (p + d) % NX
                total = total + value(d_in[pp, q, n], d_in_s[pp, q, n])
            i = q * GC + n
            sum_c[i], sum_s[i] = code(total)
            spread(1, sum_c, sum_s, i)

    for which in (0, 1):

        @pl.loop(1, NP)
        def _(d):
            i = (j + d) % NP
            wait_for(part.at[which, i], pr.at[0, which, i])
            wait_for(part_s.at[which, i], pr.at[1, which, i])

        for i in range(NP):
            part_f[i] = value(part[which, i], part_s[which, i])

        @pl.loop(0, NB)
        def _(k):
            total = acc[k] if which else jnp.zeros((A, L), F32)
            for i in range(NP):
                total = total + jnp.where(tab[which, i] == k, part_f[i], 0.0)
            acc[k] = total
            if which:
                acc_c[k], acc_s[k] = code(total)

    acc_c[NB], acc_s[NB] = code(jnp.zeros((A, L), F32))

    @pl.loop(1, NZ)
    def _(n):
        d = NZ // 2 + n // 2 * (2 * ((n - 1) % 2) - 1)
        zz = (z + d) % NZ
        two = pl.ds(first_of(zz), 2)
        send(acc_c.at[two], q_in.at[z], qs.at[0, d], qr.at[0, z], along_z(zz))
        send(acc_s.at[two], q_in_s.at[z], qs.at[1, d], qr.at[1, z], along_z(zz))

    f_own[0] = acc[mine_first]
    f_own[1] = acc[jnp.minimum(mine_first + 1, NB - 1)]

    @pl.loop(1, NZ)
    def _(d):
        zz = (z + NZ - d) % NZ
        wait_for(q_in.at[zz], qr.at[0, zz])
        wait_for(q_in_s.at[zz], qr.at[1, zz])
        f_own[...] += value(q_in[zz], q_in_s[zz])

    for e in range(2):
        h, here = chunk_at(e)
        i_lo = (L * h) // W
        i_hi = (L * h + L - 1) // W
        for n, i, live in ((0, i_lo, here), (1, i_hi, here & (i_hi != i_lo))):
            s = h - (W * i) // L

            @pl.when(live & (i == j))
            def _():
                o_in[s] = f_own[e]

            @pl.when(live & (i != j))
            def _():
                send(f_own.at[e], o_in.at[s], os_.at[e, n], or_.at[s], plane(i))

    for s in range(3):
        h = h0 + s
        block, rest = div(CP * z + h, NP), rem(CP * z + h, NP)
        holder = rem(rest + div(L * NP * block, W) + NP - SH, NP)

        @pl.when((L * h < W * (j + 1)) & (holder != j))
        def _():
            wait_for(o_in.at[s], or_.at[s])

    shifted = side_by_side([o_in[s] for s in range(3)])
    out_ref[...] = pltpu.roll(shifted, rem(3 * L - off, 3 * L), 1)[:, :W]

    for s in range(3):
        h = h0 + s

        block, rest = div(CP * z + h, NP), rem(CP * z + h, NP)
        holder = rem(rest + div(L * NP * block, W) + NP - SH, NP)

        @pl.when((L * h < W * (j + 1)) & (holder != j))
        def _():
            wait_for(img.at[s], s1s.at[s])

    @pl.loop(1, NZ)
    def _(d):
        wait_for(own, s2s.at[d])
        wait_for(q_in.at[0], qs.at[0, d])
        wait_for(q_in_s.at[0], qs.at[1, d])

    @pl.loop(0, NP)
    def _(i):
        @pl.when(i != j)
        def _():
            wait_for(s3s.at[0, i], s3as.at[i])
            wait_for(s3s.at[1, i], s3bs.at[i])
            for which in range(2):
                wait_for(part.at[which, i], ps.at[0, which, i])
                wait_for(part_s.at[which, i], ps.at[1, which, i])

        @pl.loop(1, NX)
        def _(d):
            wait_for(bop.at[i, p], s4bs.at[i, d])

    @pl.loop(1, NX)
    def _(d):
        wait_for(aop.at[p], s4as.at[d])
        wait_for(m_c.at[p], ms.at[0, d])
        wait_for(m_s.at[p], ms.at[1, d])

        @pl.loop(0, G)
        def _(q):
            wait_for(d_c.at[q, p], ds.at[0, q, d])
            wait_for(d_s.at[q, p], ds.at[1, q, d])

    for e in range(2):
        h, here = chunk_at(e)
        i_lo = (L * h) // W
        i_hi = (L * h + L - 1) // W
        for n, i, live in ((0, i_lo, here), (1, i_hi, here & (i_hi != i_lo))):

            @pl.when(live & (i != j))
            def _():
                wait_for(f_own.at[e], os_.at[e, n])


def body(n_tile, n_panel, reconstructor, c_as, tiles, tile_pairs, tile_slot):
    A, W = reconstructor.shape
    TS = tiles.shape[2]
    NX = n_panel
    NP = TS // L
    NZ = n_tile // NP
    NB = n_tile * W // TS
    T = tile_slot.shape[0]
    H = TS // NX
    G = NX
    GC = NP // G
    V = pltpu.VMEM
    D = pltpu.SemaphoreType.DMA
    cfg = (A, W, NX, NZ, NP, NB, T)
    product = pl.pallas_call(
        functools.partial(kernel, cfg),
        out_shape=jax.ShapeDtypeStruct((A, W), F32),
        in_specs=[
            pl.BlockSpec(memory_space=pltpu.SMEM),
            pl.BlockSpec(memory_space=pltpu.SMEM),
            pl.BlockSpec(memory_space=pltpu.VMEM),
            pl.BlockSpec(memory_space=pl.ANY),
        ],
        out_specs=pl.BlockSpec(memory_space=pltpu.VMEM),
        scratch_shapes=[
            V((NP, H, L), BF16),
            V((A, 3 * L), F32),
            V((3, A, L), BF16),
            V((2, 2, A, L), BF16),
            V((2, A, L), BF16),
            V((2 * NZ, A, L), BF16),
            V((2, NP, A, L), BF16),
            V((NP, A, L), BF16), V((NP, A, L), BF16),
            V((NX, GC, A, L), BF16),
            V((NP, NX, A, L), BF16),
            V((G, GC, A, L), F32),
            V((G, NX, GC, A, L), I16), V((G, NX, GC, 1, L), F32),
            V((NX, GC, A, L), I16), V((NX, GC, 1, L), F32),
            V((NX, G, GC, A, L), I16), V((NX, G, GC, 1, L), F32),
            V((NP, A, L), I16), V((NP, 1, L), F32),
            V((NP, A, L), I16), V((NP, 1, L), F32),
            V((NP, A, L), I16), V((NP, 1, L), F32),
            V((2, NP, A, L), I16), V((2, NP, 1, L), F32),
            V((NP, A, L), F32),
            V((NB, A, L), F32),
            V((NB + 1, A, L), I16), V((NB + 1, 1, L), F32),
            V((NZ, 2, A, L), I16), V((NZ, 2, 1, L), F32),
            V((2, A, L), F32),
            V((3, A, L), F32),
            pltpu.SMEM((2, NP), jnp.int32), pltpu.SMEM((2, NP), jnp.int32),
            D(()),
            pltpu.SemaphoreType.REGULAR, pltpu.SemaphoreType.REGULAR,
            D((3,)), D((2, 2)),
            D((NZ,)), D((NZ,)),
            D((NP,)), D((NP,)),
            D((NP,)), D((NP,)),
            D((NX,)), D((NX,)),
            D((NP, NX)), D((NP, NX)),
            D((2, G, NX)), D((2, G, NX)),
            D((2, NX)), D((2, NX)),
            D((2, 2, NP)), D((2, 2, NP)),
            D((2, NZ)), D((2, NZ)),
            D((2, 2)), D((3,)),
        ],
        compiler_params=pltpu.CompilerParams(
            collective_id=0, has_side_effects=True, vmem_limit_bytes=60 * 1024 * 1024
        ),
    )(tile_pairs.T, tile_slot, reconstructor, tiles)
    return 2.0 * (product - c_as.astype(F32))


def solution(mesh):
    return jax.shard_map(
        functools.partial(body, mesh.shape["tile"], mesh.shape["panel"]),
        mesh=mesh,
        in_specs=(P("panel", "tile"), P("panel", "tile"), P("tile", "panel", None), P(), P()),
        out_specs=P("panel", "tile"),
        check_vma=False,
    )
```

```python
import functools

import jax
import jax.numpy as jnp
from jax import lax
from jax.experimental import pallas as pl
from jax.experimental.pallas import tpu as pltpu
from jax.sharding import PartitionSpec as P

MESH = pl.DeviceIdType.MESH
L = 128
F32 = jnp.float32
BF16 = jnp.bfloat16
I16 = jnp.int16


def wait_for(ref, sem):
    pltpu.make_async_copy(ref, ref, sem).wait()


def div(x, n):
    return lax.div(x, jnp.int32(n))


def rem(x, n):
    return lax.rem(x, jnp.int32(n))


def code(v):
    top = jnp.maximum(jnp.max(jnp.abs(v), axis=-2, keepdims=True), 1e-30)
    return jnp.round(v * (32767.0 / top)).astype(jnp.int32).astype(jnp.int16), top * (1.0 / 32767.0)


def value(codes, scale):
    return codes.astype(jnp.int32).astype(F32) * scale


def kernel(
    cfg,
    pairs_ref, slot_ref, r_ref, x_hbm,
    out_ref,
    xv, wide, img, c_in, own, gath, s3s, afull, a_in_order, aop, bop, d_own, d_c, d_s, m_c, m_s, d_in, d_in_s, sum_c, sum_s,
    m_in, m_in_s, m_out, m_out_s, part, part_s, part_f, acc, acc_c, acc_s, q_in, q_in_s, f_own, o_in, tab, place,
    x_sem, passed_z, passed_plane, s1s, s1r, s2s, s2r, s3as, s3ar, s3bs, s3br, s4as, s4ar, s4bs, s4br,
    ds, dr, ms, mr, ps, pr, qs, qr, os_, or_,
):
    A, W, NX, NZ, NP, NB, T = cfg
    TS = NP * L
    H = TS // NX
    CP = NP * W // L
    G = NX
    GC = NP // G
    t = lax.axis_index("tile")
    p = lax.axis_index("panel")
    z = t // NP
    j = t % NP

    def plane(i):
        return {"tile": z * NP + i}

    def along_z(zz):
        return {"tile": zz * NP + j}

    def along_x(pp):
        return {"panel": pp}

    def far_first(n):
        return NP // 2 + (n + 1) // 2 * (2 * (n % 2) - 1)

    def near_first(n):
        return far_first(NP - 2 - n)


    def send(src, dst, ssem, rsem, dev):
        pltpu.make_async_remote_copy(
            src_ref=src, dst_ref=dst, send_sem=ssem, recv_sem=rsem, device_id=dev, device_id_type=MESH
        ).start()

    SH = (NP * (W - L) // W) // 2
    BIG = NP * (1 + L * NB // W)

    def chunk_no(k, pos):
        return NP * k + rem(pos + SH + BIG - div(L * NP * k, W), NP)

    def slot_of(k, pos):
        zz = div(chunk_no(k, pos), CP)
        return zz, jnp.where((k > 0) & (chunk_no(k - 1, pos) >= CP * zz), 1, 0)

    def first_of(zz):
        k = div(CP * zz, NP)
        return k + jnp.where(chunk_no(k, j) < CP * zz, 1, 0)


    c_in[...] = jnp.zeros_like(c_in)
    o_in[...] = jnp.zeros_like(o_in)
    barrier = pltpu.get_barrier_semaphore()

    REACH = 2
    CHIPS = NP // 2
    near_plane = 2 * min(CHIPS, 2 * REACH + 1) - 1
    near_z = min(NZ, 2 * REACH + 1) - 1

    def tell_plane(sem):
        for away in range(-min(REACH, (CHIPS - 1) // 2), min(REACH, CHIPS // 2) + 1):
            for core in range(2):
                i = 2 * ((j // 2 + away + CHIPS) % CHIPS) + core

                @pl.when(i != j)
                def _():
                    pl.semaphore_signal(sem, inc=1, device_id=plane(i), device_id_type=MESH)

    def tell_z(sem):
        for d in range(1, NZ):
            if min(d, NZ - d) <= REACH:
                pl.semaphore_signal(sem, inc=1, device_id=along_z((z + d) % NZ), device_id_type=MESH)

    tell_plane(barrier)
    tell_z(barrier)

    @pl.loop(1, NX)
    def _(d):
        pl.semaphore_signal(barrier, inc=1, device_id=along_x((p + d) % NX), device_id_type=MESH)

    h0 = (W * j) // L
    off = W * j - L * h0
    wide[...] = jnp.zeros_like(wide)
    wide[:, :W] = r_ref[...].astype(F32)
    placed = pltpu.roll(wide[...], off, 1).astype(BF16)
    for s in range(3):
        img[s] = placed[:, s * L : (s + 1) * L]

    pl.semaphore_wait(barrier, near_plane + near_z + NX - 1)

    for s in range(3):
        h = h0 + s
        live = L * h < W * (j + 1)
        block, rest = div(CP * z + h, NP), rem(CP * z + h, NP)
        dest = rem(rest + div(L * NP * block, W) + NP - SH, NP)
        _, e = slot_of(block, dest)
        c = jnp.where((off > 0) & (s == 0), 1, 0)

        @pl.when(live & (dest == j))
        def _():
            c_in[e, c] = img[s]

        @pl.when(live & (dest != j))
        def _():
            send(img.at[s], c_in.at[e, c], s1s.at[s], s1r.at[e, c], plane(dest))

    tell_z(passed_z)
    tell_plane(passed_plane)

    for i in range(NP):
        pltpu.make_async_copy(x_hbm.at[0, :, pl.ds(i * L, L)], xv.at[i], x_sem).start()

    mine_first = first_of(z)

    def chunk_at(e):
        h = chunk_no(mine_first + e, j) - CP * z
        return h, (mine_first + e < NB) & (h < CP)

    for e in range(2):
        h, live = chunk_at(e)
        i_lo = (L * h) // W
        i_hi = (L * h + L - 1) // W

        @pl.when(live & (i_lo != j))
        def _():
            wait_for(c_in.at[e, 0], s1r.at[e, 0])

        @pl.when(live & (i_hi != i_lo) & (i_hi != j))
        def _():
            wait_for(c_in.at[e, 1], s1r.at[e, 1])

        mix = (c_in[e, 0].astype(F32) + c_in[e, 1].astype(F32)).astype(BF16)
        own[e] = mix
        gath[2 * z + e] = mix

    pl.semaphore_wait(passed_z, near_z)
    @pl.loop(1, NZ)
    def _(n):
        d = NZ // 2 + n // 2 * (2 * ((n - 1) % 2) - 1)
        zz = (z + d) % NZ
        send(own, gath.at[pl.ds(2 * z, 2)], s2s.at[d], s2r.at[z], along_z(zz))

    def look(n, got):
        slot = slot_ref[n]
        code = pairs_ref[0, n] * 16 + pairs_ref[1, n]
        return tuple(jnp.where(slot == z * NP + i, code, got[i]) for i in range(NP))

    found = lax.fori_loop(0, T, look, tuple(jnp.int32(-1) for _ in range(NP)))
    mine = jnp.int32(-1)
    for i in range(NP):
        known = jnp.maximum(found[i], 0)
        for which, block in enumerate((known // 16, known % 16)):
            tab[which, i] = block
            zz, e = slot_of(block, j)
            place[which, i] = 2 * zz + e
        mine = jnp.where(j == i, found[i], mine)
    known = jnp.maximum(mine, 0)
    turn_a = rem(div(L * NP * (known // 16), W) + NP - SH, NP)
    turn_b = rem(div(L * NP * (known % 16), W) + NP - SH, NP)
    diag = jnp.where(mine // 16 == mine % 16, 0.5, 1.0)
    factor = jnp.where(mine < 0, 0.0, diag).astype(F32)

    @pl.loop(1, NZ)
    def _(d):
        zz = (z + NZ - d) % NZ
        wait_for(gath.at[pl.ds(2 * zz, 2)], s2r.at[zz])

    def chunk_of(which, i):
        return gath[place[which, i]]

    pl.semaphore_wait(passed_plane, near_plane)

    def plane_stage(which, full, ssem, rsem):
        @pl.loop(0, NP - 1)
        def _(n):
            i = (j + near_first(n)) % NP
            s3s[which, i] = chunk_of(which, i)
            send(s3s.at[which, i], full(j), ssem.at[i], rsem.at[j], plane(i))

    def b_chunk(i):
        return bop.at[i, p]

    def a_chunk(i):
        return afull.at[i]

    plane_stage(1, b_chunk, s3bs, s3br)
    bop[j, p] = chunk_of(1, j)
    plane_stage(0, a_chunk, s3as, s3ar)
    afull[j] = chunk_of(0, j)

    def pair(c, pp):
        return bop.at[pl.ds(2 * c, 2), pp]

    def forward(c):
        @pl.loop(1, NX)
        def _(d):
            send(pair(c, p), pair(c, p), s4bs.at[c, d], s4br.at[c, p], along_x((p + d) % NX))

    other = j + 1 - 2 * (j % 2)
    wait_for(bop.at[other, p], s3br.at[other])
    forward(j // 2)

    @pl.loop(0, CHIPS - 1)
    def _(n):
        m = CHIPS - 2 - n
        away = CHIPS // 2 + (m + 1) // 2 * (2 * (m % 2) - 1)
        c = (j // 2 + CHIPS - away) % CHIPS
        wait_for(bop.at[2 * c, p], s3br.at[2 * c])
        wait_for(bop.at[2 * c + 1, p], s3br.at[2 * c + 1])
        forward(c)

    wait_for(xv, x_sem)

    def x_chunk(i):
        return xv[rem(i + NP - turn_b, NP)]

    def side_by_side(pieces):
        return jnp.concatenate(pieces, axis=1)

    @pl.loop(1, NP)
    def _(d):
        i = (j + d) % NP
        wait_for(afull.at[i], s3ar.at[i])

    for i in range(NP):
        a_in_order[i] = afull[rem(i + turn_a, NP)]

    @pl.loop(1, NX)
    def _(d):
        pp = (p + d) % NX
        send(a_in_order.at[pl.ds(pp * GC, GC)], aop.at[p], s4as.at[d], s4ar.at[p], along_x(pp))

    aop[p] = a_in_order[pl.ds(p * GC, GC)]

    prod = jnp.zeros((A * NX, H), F32)
    for q in range(G):

        @pl.loop(1, NX)
        def _(d):
            pp = (p + d) % NX

            @pl.loop(q * GC // 2, (q + 1) * GC // 2)
            def _(c):
                wait_for(pair(c, pp), s4br.at[c, pp])

        b_cols = side_by_side([bop[q * GC + n].reshape(NX * A, L) for n in range(GC)])
        x_cols = side_by_side([x_chunk(q * GC + n) for n in range(GC)])
        prod = prod + lax.dot_general(b_cols, x_cols, (((1,), (1,)), ((), ())), preferred_element_type=F32)
    prod = prod * factor
    for pp in range(NX):
        for n in range(GC):
            m_c[pp, n], m_s[pp, n] = code(prod[pp * A : (pp + 1) * A, n * L : (n + 1) * L])

    own_chunks = pl.ds(p * GC, GC)

    @pl.loop(1, NX)
    def _(d):
        pp = (p + d) % NX
        send(m_c.at[pp], m_in.at[own_chunks], ms.at[0, d], mr.at[0, p], along_x(pp))
        send(m_s.at[pp], m_in_s.at[own_chunks], ms.at[1, d], mr.at[1, p], along_x(pp))

    m_in[own_chunks] = m_c[p]
    m_in_s[own_chunks] = m_s[p]

    @pl.loop(1, NX)
    def _(d):
        pp = (p + d) % NX
        wait_for(aop.at[pp], s4ar.at[pp])

    a_rows = jnp.concatenate([side_by_side([aop[pp, n] for n in range(GC)]) for pp in range(NX)], axis=0)

    def group(n):
        return (n + j // GC) % G

    @pl.loop(0, G)
    def _(step):
        q = group(step)
        x_cols = side_by_side([x_chunk(q * GC + n) for n in range(GC)])
        prod = jnp.dot(a_rows, x_cols, preferred_element_type=F32) * factor
        for pp in range(NX):
            for n in range(GC):
                v = prod[pp * A : (pp + 1) * A, n * L : (n + 1) * L]
                d_c[q, pp, n], d_s[q, pp, n] = code(v)

                @pl.when(p == pp)
                def _():
                    d_own[q, n] = v

        @pl.loop(1, NX)
        def _(d):
            pp = (p + d) % NX
            send(d_c.at[q, pp], d_in.at[p, q], ds.at[0, q, d], dr.at[0, q, p], along_x(pp))
            send(d_s.at[q, pp], d_in_s.at[p, q], ds.at[1, q, d], dr.at[1, q, p], along_x(pp))

    def spread(which, codes, scales, i):
        @pl.when(i != j)
        def _():
            send(codes.at[i], part.at[which, j], ps.at[0, which, i], pr.at[0, which, j], plane(i))
            send(scales.at[i], part_s.at[which, j], ps.at[1, which, i], pr.at[1, which, j], plane(i))

        @pl.when(i == j)
        def _():
            part[which, j] = codes[i]
            part_s[which, j] = scales[i]

    @pl.loop(1, NX)
    def _(d):
        pp = (p + d) % NX
        wait_for(m_in.at[pl.ds(pp * GC, GC)], mr.at[0, pp])
        wait_for(m_in_s.at[pl.ds(pp * GC, GC)], mr.at[1, pp])

    @pl.loop(0, NP)
    def _(n):
        i = (j + far_first(n)) % NP
        r = rem(i + NP - turn_a, NP)
        m_out[i] = m_in[r]
        m_out_s[i] = m_in_s[r]
        spread(0, m_out, m_out_s, i)

    @pl.loop(0, G)
    def _(step):
        q = group(step)

        @pl.loop(1, NX)
        def _(d):
            pp = (p + d) % NX
            wait_for(d_in.at[pp, q], dr.at[0, q, pp])
            wait_for(d_in_s.at[pp, q], dr.at[1, q, pp])

        @pl.loop(0, GC)
        def _(turn):
            n = (turn + j) % GC
            total = d_own[q, n]
            for d in range(1, NX):
                pp = (p + d) % NX
                total = total + value(d_in[pp, q, n], d_in_s[pp, q, n])
            i = q * GC + n
            sum_c[i], sum_s[i] = code(total)
            spread(1, sum_c, sum_s, i)

    for which in (0, 1):

        @pl.loop(1, NP)
        def _(d):
            i = (j + d) % NP
            wait_for(part.at[which, i], pr.at[0, which, i])
            wait_for(part_s.at[which, i], pr.at[1, which, i])

        for i in range(NP):
            part_f[i] = value(part[which, i], part_s[which, i])

        @pl.loop(0, NB)
        def _(k):
            total = acc[k] if which else jnp.zeros((A, L), F32)
            for i in range(NP):
                total = total + jnp.where(tab[which, i] == k, part_f[i], 0.0)
            acc[k] = total
            if which:
                acc_c[k], acc_s[k] = code(total)

    acc_c[NB], acc_s[NB] = code(jnp.zeros((A, L), F32))

    @pl.loop(1, NZ)
    def _(n):
        d = NZ // 2 + n // 2 * (2 * ((n - 1) % 2) - 1)
        zz = (z + d) % NZ
        two = pl.ds(first_of(zz), 2)
        send(acc_c.at[two], q_in.at[z], qs.at[0, d], qr.at[0, z], along_z(zz))
        send(acc_s.at[two], q_in_s.at[z], qs.at[1, d], qr.at[1, z], along_z(zz))

    f_own[0] = acc[mine_first]
    f_own[1] = acc[jnp.minimum(mine_first + 1, NB - 1)]

    @pl.loop(1, NZ)
    def _(d):
        zz = (z + NZ - d) % NZ
        wait_for(q_in.at[zz], qr.at[0, zz])
        wait_for(q_in_s.at[zz], qr.at[1, zz])
        f_own[...] += value(q_in[zz], q_in_s[zz])

    for e in range(2):
        h, here = chunk_at(e)
        i_lo = (L * h) // W
        i_hi = (L * h + L - 1) // W
        for n, i, live in ((0, i_lo, here), (1, i_hi, here & (i_hi != i_lo))):
            s = h - (W * i) // L

            @pl.when(live & (i == j))
            def _():
                o_in[s] = f_own[e]

            @pl.when(live & (i != j))
            def _():
                send(f_own.at[e], o_in.at[s], os_.at[e, n], or_.at[s], plane(i))

    for s in range(3):
        h = h0 + s
        block, rest = div(CP * z + h, NP), rem(CP * z + h, NP)
        holder = rem(rest + div(L * NP * block, W) + NP - SH, NP)

        @pl.when((L * h < W * (j + 1)) & (holder != j))
        def _():
            wait_for(o_in.at[s], or_.at[s])

    shifted = side_by_side([o_in[s] for s in range(3)])
    out_ref[...] = pltpu.roll(shifted, rem(3 * L - off, 3 * L), 1)[:, :W]

    for s in range(3):
        h = h0 + s

        block, rest = div(CP * z + h, NP), rem(CP * z + h, NP)
        holder = rem(rest + div(L * NP * block, W) + NP - SH, NP)

        @pl.when((L * h < W * (j + 1)) & (holder != j))
        def _():
            wait_for(img.at[s], s1s.at[s])

    @pl.loop(1, NZ)
    def _(d):
        wait_for(own, s2s.at[d])
        wait_for(q_in.at[0], qs.at[0, d])
        wait_for(q_in_s.at[0], qs.at[1, d])

    @pl.loop(0, NP)
    def _(i):
        @pl.when(i != j)
        def _():
            wait_for(s3s.at[0, i], s3as.at[i])
            wait_for(s3s.at[1, i], s3bs.at[i])
            for which in range(2):
                wait_for(part.at[which, i], ps.at[0, which, i])
                wait_for(part_s.at[which, i], ps.at[1, which, i])

    @pl.loop(0, CHIPS)
    def _(c):
        @pl.loop(1, NX)
        def _(d):
            wait_for(pair(c, p), s4bs.at[c, d])

    @pl.loop(1, NX)
    def _(d):
        wait_for(aop.at[p], s4as.at[d])
        wait_for(m_c.at[p], ms.at[0, d])
        wait_for(m_s.at[p], ms.at[1, d])

        @pl.loop(0, G)
        def _(q):
            wait_for(d_c.at[q, p], ds.at[0, q, d])
            wait_for(d_s.at[q, p], ds.at[1, q, d])

    for e in range(2):
        h, here = chunk_at(e)
        i_lo = (L * h) // W
        i_hi = (L * h + L - 1) // W
        for n, i, live in ((0, i_lo, here), (1, i_hi, here & (i_hi != i_lo))):

            @pl.when(live & (i != j))
            def _():
                wait_for(f_own.at[e], os_.at[e, n])


def body(n_tile, n_panel, reconstructor, c_as, tiles, tile_pairs, tile_slot):
    A, W = reconstructor.shape
    TS = tiles.shape[2]
    NX = n_panel
    NP = TS // L
    NZ = n_tile // NP
    NB = n_tile * W // TS
    T = tile_slot.shape[0]
    H = TS // NX
    G = NX
    GC = NP // G
    V = pltpu.VMEM
    D = pltpu.SemaphoreType.DMA
    cfg = (A, W, NX, NZ, NP, NB, T)
    product = pl.pallas_call(
        functools.partial(kernel, cfg),
        out_shape=jax.ShapeDtypeStruct((A, W), F32),
        in_specs=[
            pl.BlockSpec(memory_space=pltpu.SMEM),
            pl.BlockSpec(memory_space=pltpu.SMEM),
            pl.BlockSpec(memory_space=pltpu.VMEM),
            pl.BlockSpec(memory_space=pl.ANY),
        ],
        out_specs=pl.BlockSpec(memory_space=pltpu.VMEM),
        scratch_shapes=[
            V((NP, H, L), BF16),
            V((A, 3 * L), F32),
            V((3, A, L), BF16),
            V((2, 2, A, L), BF16),
            V((2, A, L), BF16),
            V((2 * NZ, A, L), BF16),
            V((2, NP, A, L), BF16),
            V((NP, A, L), BF16), V((NP, A, L), BF16),
            V((NX, GC, A, L), BF16),
            V((NP, NX, A, L), BF16),
            V((G, GC, A, L), F32),
            V((G, NX, GC, A, L), I16), V((G, NX, GC, 1, L), F32),
            V((NX, GC, A, L), I16), V((NX, GC, 1, L), F32),
            V((NX, G, GC, A, L), I16), V((NX, G, GC, 1, L), F32),
            V((NP, A, L), I16), V((NP, 1, L), F32),
            V((NP, A, L), I16), V((NP, 1, L), F32),
            V((NP, A, L), I16), V((NP, 1, L), F32),
            V((2, NP, A, L), I16), V((2, NP, 1, L), F32),
            V((NP, A, L), F32),
            V((NB, A, L), F32),
            V((NB + 1, A, L), I16), V((NB + 1, 1, L), F32),
            V((NZ, 2, A, L), I16), V((NZ, 2, 1, L), F32),
            V((2, A, L), F32),
            V((3, A, L), F32),
            pltpu.SMEM((2, NP), jnp.int32), pltpu.SMEM((2, NP), jnp.int32),
            D(()),
            pltpu.SemaphoreType.REGULAR, pltpu.SemaphoreType.REGULAR,
            D((3,)), D((2, 2)),
            D((NZ,)), D((NZ,)),
            D((NP,)), D((NP,)),
            D((NP,)), D((NP,)),
            D((NX,)), D((NX,)),
            D((NP // 2, NX)), D((NP // 2, NX)),
            D((2, G, NX)), D((2, G, NX)),
            D((2, NX)), D((2, NX)),
            D((2, 2, NP)), D((2, 2, NP)),
            D((2, NZ)), D((2, NZ)),
            D((2, 2)), D((3,)),
        ],
        compiler_params=pltpu.CompilerParams(
            collective_id=0, has_side_effects=True, vmem_limit_bytes=60 * 1024 * 1024
        ),
    )(tile_pairs.T, tile_slot, reconstructor, tiles)
    return 2.0 * (product - c_as.astype(F32))


def solution(mesh):
    return jax.shard_map(
        functools.partial(body, mesh.shape["tile"], mesh.shape["panel"]),
        mesh=mesh,
        in_specs=(P("panel", "tile"), P("panel", "tile"), P("tile", "panel", None), P(), P()),
        out_specs=P("panel", "tile"),
        check_vma=False,
    )
```
